512 devices in a mesh: section: 64 (over y, z_hi, core), tp: 8 (over z_lo, x).
Axes of the slice: x: 4, y: 8, z: 8 (z_hi: 4, z_lo: 2; z = z_hi * 2 + z_lo), core: 2. Of those that a mesh axis runs over, the one named last changes fastest.
Arguments:
- arriving: bfloat16 [64, 96, 2048], P('section'), may hold values from -10.8 to 10.8
- norm_gain: bfloat16 [64, 2048], P('section'), may hold values from 0.099609375 to 1.8984375
- w_qkv: bfloat16 [64, 2048, 3072], P('section', None, 'tp'), may hold values from -0.09375 to 0.09375
- w_out: bfloat16 [64, 2048, 2048], P('section', 'tp'), may hold values from -0.125 to 0.125
- cache: bfloat16 [64, 4, 48, 16, 1024], P('section', None, None, None, 'tp')
- lengths: int32 [32, 96], replicated, may hold values from 1 to 16, as said below
- talk_gain: bfloat16 [2, 2048], P(None, 'tp'), may hold values from 0.5 to 1.5
- w_adapt: bfloat16 [2, 2048, 3072], P(None, 'tp', 'section'), may hold values from -0.09375 to 0.09375
- codebooks: bfloat16 [4, 2048, 3072], P(None, 'tp', 'section'), may hold values from -3 to 3
- codes: int32 [4, 96, 4], replicated, may hold values from 0 to 2048, as said below
Outputs:
- leaving: float32 [64, 96, 2048], P('section')
- talker_in: float32 [4, 96, 3072], P(None, None, 'section')
The draws below stay inside these ranges and needn't reach their ends.
Inputs may be any that keep to these rules, and one draw needn't show every extreme that they name: `lengths`: every micro-batch holds one or more streams of length 16. 2048 marks a codebook not yet started under the delay pattern: if codes[k, b, q] is 2048, so is codes[k, b, q'] for every q' > q.
All inputs are finite; a program needn't handle non-finite values.
Results may differ from the reference program's by a relative error of at most 0.034.
Values may be sent and summed in bfloat16 or wider, within the bound.
No kernel may reach another device: no remote copies, remote signals or barrier semaphores. Data moves between devices by JAX's collectives and lax.ppermute only.
A program may use at most 64 MiB of HBM per device.

```python
import math
import jax
import jax.numpy as jnp
from jax import lax

D = 4096
H = 32
KVH = 8
HD = 64
DT = 3072
NQ = 4
VC = 2048
TICKS = 4
B = 96
CACHE = 16
PIPE = 32
N_SECTION = 64


def draw_arriving(key, part):
    key = jax.random.fold_in(key, 5)
    key_values = jax.random.fold_in(key, 0)
    feature_pos = jnp.arange(D // 2, dtype=jnp.float32) / (D // 2 - 1)
    feature_scale = jnp.exp(math.log(0.6) + feature_pos * math.log(3.0))
    values = jnp.clip(jax.random.normal(key_values, (2 * PIPE, B, D // 2), jnp.float32), -6.0, 6.0)
    return (values * feature_scale[None, None, :]).astype(jnp.bfloat16)


def draw_cache(key, part):
    key = jax.random.fold_in(key, 11)
    key_values = jax.random.fold_in(key, 0)
    normal_draw = jax.random.normal(key_values, (2 * PIPE, TICKS, B // 2, CACHE, KVH, 2, HD), jnp.float32)
    return normal_draw.reshape(2 * PIPE, TICKS, B // 2, CACHE, KVH * 2 * HD).astype(jnp.bfloat16)


def draw_lengths(key, part):
    key = jax.random.fold_in(key, 23)
    key_length, key_pick = jax.random.split(key)
    stream_lens = jax.random.randint(key_length, (PIPE, B), 1, CACHE + 1)
    pick_row = jax.random.randint(key_pick, (PIPE, 1), 0, B)
    at_most = jnp.arange(B)[None, :] == pick_row
    return jnp.where(at_most, CACHE, stream_lens).astype(jnp.int32)


def draw_codes(key, part):
    key = jax.random.fold_in(key, 37)
    key_frame, key_token, key_pick = jax.random.split(key, 3)
    frame_index = jax.random.randint(key_frame, (TICKS, B, 1), 0, 2 * NQ)
    pick_row = jax.random.randint(key_pick, (TICKS, 1, 1), 0, B)
    frame_index = jnp.where(jnp.arange(B)[None, :, None] == pick_row, 0, frame_index)
    token_ids = jax.random.randint(key_token, (TICKS, B, NQ), 0, VC)
    book_index = jnp.arange(NQ)[None, None, :]
    return jnp.where(frame_index >= book_index, token_ids, VC).astype(jnp.int32)


def level_of(rng, dims, cuts, smallest, top_value):
    def one(position, blocks):
        steps = jax.random.uniform(jax.random.fold_in(jax.random.fold_in(rng, 6), position), (blocks,), jnp.float32, smallest / len(cuts), top_value / len(cuts))
        return jnp.repeat(jnp.exp(steps), dims[position] // blocks).reshape((-1,) + (1,) * (len(dims) - position - 1))

    loudness = one(*cuts[0])
    for cut in cuts[1:]:
        loudness = loudness * one(*cut)
    return loudness


def noise(rng, dims, spread, most, pieces=(), held_as=jnp.bfloat16):
    result = spread * jax.random.normal(rng, dims, jnp.float32)
    if pieces:
        result = result * level_of(rng, dims, pieces, -0.22, 0.18)
    return jnp.clip(result, -most, most).astype(held_as)


def setup_inputs(seed: int = 0) -> dict:
    seeds = jax.random.split(jax.random.key(seed), 11)
    arriving = draw_arriving(jax.random.fold_in(seeds[10], 71), 0)
    norm_gain = jnp.clip(1.0 + 0.18 * jax.random.normal(seeds[1], (2 * PIPE, D // 2), jnp.float32), 0.099609375, 1.8984375).astype(jnp.bfloat16)
    w_qkv = noise(seeds[2], (2 * PIPE, D // 2, KVH * (H // KVH + 2) * HD), D ** -0.5, 0.09375, ((0, 64), (2, 8)))
    w_out = noise(seeds[3], (2 * PIPE, H * HD, D // 2), (H * HD) ** -0.5, 0.125, ((0, 64), (1, 8)))
    cache = draw_cache(jax.random.fold_in(seeds[10], 71), 0)
    lengths = draw_lengths(jax.random.fold_in(seeds[10], 71), 0)
    talk_gain = jnp.clip(1.0 + 0.1 * jax.random.normal(seeds[6], (2, D // 2), jnp.float32), 0.5, 1.5).astype(jnp.bfloat16)
    w_adapt = noise(seeds[7], (2, D // 2, DT), D ** -0.5, 0.09375, ((1, 8), (2, 64)))
    codebooks = noise(seeds[8], (NQ, VC, DT), 0.5, 3.0, ((1, 8), (2, 64)))
    codes = draw_codes(jax.random.fold_in(seeds[10], 71), 0)
    return dict(arriving=arriving, norm_gain=norm_gain, w_qkv=w_qkv, w_out=w_out, cache=cache, lengths=lengths, talk_gain=talk_gain, w_adapt=w_adapt, codebooks=codebooks, codes=codes)


epsilon = 1e-05

def attend(queries, keys_new, values_new, cached_now, stream_lens):
    cache_keys = cached_now[:, :, :, 0, :].astype(jnp.float32)
    cache_values = cached_now[:, :, :, 1, :].astype(jnp.float32)
    query_f = queries.astype(jnp.float32)
    score_scale = 1.0 / math.sqrt(HD)
    scores = jnp.einsum('bgrd,bjgd->bgrj', query_f, cache_keys) * score_scale
    own_score = jnp.einsum('bgrd,bgd->bgr', query_f, keys_new.astype(jnp.float32)) * score_scale
    visible = (jnp.arange(CACHE)[None, :] < stream_lens[:, None])[:, None, None, :]
    row_max = jnp.maximum(lax.optimization_barrier(jnp.max(jnp.where(visible, scores, -jnp.inf), axis=-1)), own_score)
    weights = jnp.where(visible, jnp.exp(scores - row_max[..., None]), 0.0)
    own_weight = jnp.exp(own_score - row_max)
    denom_sum = lax.optimization_barrier(jnp.sum(weights, axis=-1)) + own_weight
    weights = (weights / denom_sum[..., None]).astype(jnp.bfloat16)
    own_weight = (own_weight / denom_sum).astype(jnp.bfloat16)
    mixed_out = jnp.einsum('bgrj,bjgd->bgrd', weights.astype(jnp.float32), cache_values)
    mixed_out = mixed_out + own_weight.astype(jnp.float32)[..., None] * values_new.astype(jnp.float32)[:, :, None, :]
    return mixed_out.astype(jnp.bfloat16)

def apply_layer(entry_rows, section_gain, qkv_weight, out_weight, cached_now, stream_lens):
    head_ratio = H // KVH
    rows_f = entry_rows.astype(jnp.float32)
    inv_rms = lax.rsqrt(lax.optimization_barrier(jnp.mean(rows_f * rows_f, axis=-1)) + epsilon)
    scaled = (rows_f * section_gain.astype(jnp.float32)).astype(jnp.bfloat16)
    mixed_proj = jnp.dot(scaled, qkv_weight, preferred_element_type=jnp.float32) * inv_rms[:, None]
    mixed_proj = mixed_proj.reshape(B, KVH, head_ratio + 2, HD)
    queries = mixed_proj[:, :, :head_ratio].astype(jnp.bfloat16)
    keys_new = mixed_proj[:, :, head_ratio].astype(jnp.bfloat16)
    values_new = mixed_proj[:, :, head_ratio + 1].astype(jnp.bfloat16)
    head_rows = attend(queries, keys_new, values_new, cached_now, stream_lens).reshape(B, H * HD)
    update = jnp.dot(head_rows, out_weight, preferred_element_type=jnp.float32)
    return rows_f + update

def talker_input(hidden, talk_gain, w_adapt, codebooks, codes_now):
    hidden_f = hidden.astype(jnp.float32)
    talk_rms = lax.rsqrt(lax.optimization_barrier(jnp.mean(hidden_f * hidden_f, axis=-1)) + epsilon)
    scaled = (hidden_f * talk_gain.reshape(D).astype(jnp.float32)).astype(jnp.bfloat16)
    adapted = jnp.dot(scaled, w_adapt.reshape(D, DT), preferred_element_type=jnp.float32) * talk_rms[:, None]
    embedded = jnp.zeros((B, DT), jnp.float32)
    for book_index in range(NQ):
        token_ids = codes_now[:, book_index]
        picked = jnp.take(codebooks[book_index], jnp.minimum(token_ids, VC - 1), axis=0).astype(jnp.float32)
        embedded = embedded + jnp.where((token_ids < VC)[:, None], picked, 0.0)
    return adapted + embedded

def reference(arriving, norm_gain, w_qkv, w_out, cache, lengths, talk_gain, w_adapt, codebooks, codes):
    sections = N_SECTION // 2
    half_width = D // 2
    entry_rows = arriving.reshape(sections, 2, B, half_width).transpose(0, 2, 1, 3).reshape(sections, B, D).astype(jnp.float32)
    section_gains = norm_gain.reshape(sections, D)
    qkv_weights = w_qkv.reshape(sections, D, -1)
    out_weights = w_out.reshape(sections, 2, H * HD, half_width).transpose(0, 2, 1, 3).reshape(sections, H * HD, D)
    cached = cache.reshape(sections, 2, TICKS, B // 2, CACHE, KVH, 2, HD)
    cached = cached.transpose(0, 2, 1, 3, 4, 5, 6, 7).reshape(sections, TICKS, B, CACHE, KVH, 2, HD)
    section_ids = jnp.arange(sections)

    def run_section(items):
        return apply_layer(*items)
    current = entry_rows
    latest = entry_rows
    talker_list = []
    for tick_index in range(TICKS):
        active = section_ids >= tick_index
        lens_now = jnp.where(active[:, None], jnp.roll(lengths, tick_index, axis=0), 0).astype(jnp.int32)
        produced = lax.map(run_section, (current, section_gains, qkv_weights, out_weights, cached[:, tick_index], lens_now))
        if tick_index == 0:
            latest = produced
        else:
            latest = jnp.where(active[:, None, None], produced, latest)
        talker_list.append(talker_input(produced[sections - 1], talk_gain, w_adapt, codebooks, codes[tick_index]))
        current = jnp.concatenate([jnp.zeros((1, B, D), jnp.float32), produced[:-1]], axis=0)
    leaving = latest.reshape(sections, B, 2, half_width).transpose(0, 2, 1, 3).reshape(2 * sections, B, half_width)
    return (leaving, jnp.stack(talker_list))
```

```python
import functools

import jax
import jax.numpy as jnp
from jax import lax
from jax.experimental import pallas as pl
from jax.experimental.pallas import tpu as pltpu
from jax.sharding import PartitionSpec as P

D = 4096
H = 32
KVH = 8
HD = 64
NQ = 4
TICKS = 4
B = 96
CACHE = 16
HALF = B // 2
RATIO = H // KVH

epsilon = 1e-05
f32 = jnp.float32
bf16 = jnp.bfloat16
VMEM = pltpu.VMEM


def section_core(tick, scaled, total_squares, hi_ref, w_own, w_oth, o_own, o_oth, cache_ref, out_ref):
    shards, block = out_ref.shape[0], out_ref.shape[2] // 2
    proj = jnp.zeros((HALF, w_own.shape[1]), f32)
    for own_rows, oth_rows, low, high in scaled:
        proj = proj + jnp.dot(own_rows, w_own[low:high, :], preferred_element_type=f32)
        proj = proj + jnp.dot(oth_rows, w_oth[low:high, :], preferred_element_type=f32)
    proj = proj * lax.rsqrt(total_squares / D + epsilon)
    stacked = jnp.concatenate([proj[:, r * HD : (r + 1) * HD] for r in range(RATIO)], axis=0)
    queries = (stacked.astype(bf16).astype(f32) * (HD**-0.5)).astype(bf16)
    queries = jnp.concatenate([queries, jnp.zeros_like(queries)], axis=1)
    pair_new = proj[:, RATIO * HD :].astype(bf16)
    pairs = cache_ref[tick]
    contract_last = (((1,), (1,)), ((), ()))
    scores = lax.dot_general(queries, pairs, contract_last, preferred_element_type=f32)
    own_scores = lax.dot_general(queries, pair_new, contract_last, preferred_element_type=f32)
    rows = RATIO * HALF
    stream = lax.rem(lax.broadcasted_iota(jnp.int32, (rows, 1), 0), HALF)
    place = lax.broadcasted_iota(jnp.int32, (rows, HALF * CACHE), 1)
    visible = jnp.logical_and(place >= stream * CACHE, place < hi_ref[tick])
    scores = jnp.where(visible, scores, -jnp.inf)
    own_place = lax.broadcasted_iota(jnp.int32, (rows, HALF), 1)
    own_scores = jnp.where(own_place == stream, own_scores, -jnp.inf)
    row_max = jnp.maximum(
        jnp.max(scores, axis=-1, keepdims=True), jnp.max(own_scores, axis=-1, keepdims=True)
    )
    weights = jnp.exp(scores - row_max)
    own_weights = jnp.exp(own_scores - row_max)
    total = jnp.sum(weights, axis=-1, keepdims=True) + jnp.sum(own_weights, axis=-1, keepdims=True)
    share = 1.0 / total
    mixed = jnp.dot((weights * share).astype(bf16), pairs, preferred_element_type=f32)
    mixed = mixed + jnp.dot(
        (own_weights * share).astype(bf16), pair_new, preferred_element_type=f32
    )
    mixed = mixed[:, HD:].astype(bf16)
    heads = jnp.concatenate([mixed[r * HALF : (r + 1) * HALF] for r in range(RATIO)], axis=1)
    for j in range(shards):
        span = slice(j * block, (j + 1) * block)
        out_ref[j, :, :block] = jnp.dot(heads, o_own[:, span], preferred_element_type=f32).astype(
            bf16
        )
        out_ref[j, :, block:] = jnp.dot(heads, o_oth[:, span], preferred_element_type=f32).astype(
            bf16
        )


def first_kernel(
    tick, x_own, x_oth, g_own, g_oth, hi_ref, w_own, w_oth, o_own, o_oth, cache_ref, out_ref
):
    own = x_own[...].astype(f32)
    oth = x_oth[...].astype(f32)
    squares = jnp.sum(own * own + oth * oth, axis=-1, keepdims=True)
    scaled_own = (own * g_own[...]).astype(bf16)
    scaled_oth = (oth * g_oth[...]).astype(bf16)
    scaled = [(scaled_own, scaled_oth, 0, x_own.shape[1])]
    section_core(
        tick, scaled, squares, hi_ref, w_own, w_oth, o_own, o_oth, cache_ref, out_ref
    )


def later_kernel(tick, x_ref, inverse_gain, hi_ref, w_own, w_oth, o_own, o_oth, cache_ref, out_ref):
    shards, block = x_ref.shape[0], x_ref.shape[2] // 2
    squares = jnp.zeros(x_ref.shape[1:], f32)
    scaled = []
    for j in range(shards):
        rows = x_ref[j]
        plain = rows.astype(f32) * inverse_gain[j : j + 1, :]
        squares = squares + plain * plain
        scaled.append((rows[:, :block], rows[:, block:], j * block, (j + 1) * block))
    squares = jnp.sum(squares, axis=-1, keepdims=True)
    section_core(
        tick, scaled, squares, hi_ref, w_own, w_oth, o_own, o_oth, cache_ref, out_ref
    )


def run_kernel(kernel, shards, block, *operands):
    return pl.pallas_call(
        kernel,
        out_shape=jax.ShapeDtypeStruct((shards, HALF, 2 * block), bf16),
        in_specs=[pl.BlockSpec(memory_space=VMEM)] * len(operands),
        out_specs=pl.BlockSpec(memory_space=VMEM),
        compiler_params=pltpu.CompilerParams(vmem_limit_bytes=32 * 2**20),
    )(*operands)


def to_partner(value):
    pairs = [(i, i ^ 1) for i in range(lax.axis_size("section"))]
    return lax.ppermute(value, "section", pairs)


def to_next(value):
    count = lax.axis_size("section")
    return lax.ppermute(value, "section", [(i, i + 2) for i in range(count - 2)])


def exchange(blocks):
    return lax.all_to_all(blocks, "tp", 0, 0, tiled=True)


def gather(block):
    count = lax.axis_size("tp")
    return exchange(jnp.broadcast_to(block[None], (count,) + block.shape))


def from_last(value, position):
    count = lax.axis_size("section")
    line = 8
    base = count - line
    total = jnp.where(position // 2 == count // 2 - 1, value, jnp.zeros_like(value))
    for z in range(0, line - 2, 2):
        total = total + lax.ppermute(
            value, "section", [(count - 2 + c, base + z + c) for c in range(2)]
        )
    result = jnp.where(position >= base, total, jnp.zeros_like(value))
    for start in range(0, base, line):
        result = result + lax.ppermute(
            total, "section", [(base + i, start + i) for i in range(line)]
        )
    return result


def body(arriving, norm_gain, w_qkv, w_out, cache, lengths, talk_gain, w_adapt, codebooks, codes):
    position = lax.axis_index("section")
    column = lax.axis_index("tp")
    shards = lax.axis_size("tp")
    side = lax.rem(position, 2)
    section = position // 2
    width = arriving.shape[2]
    block = width // shards

    rows = arriving[0]
    mine = lax.dynamic_slice_in_dim(rows, side * HALF, HALF, 0)
    theirs = lax.dynamic_slice_in_dim(rows, (1 - side) * HALF, HALF, 0)
    got = to_partner(jnp.concatenate([theirs, norm_gain], axis=0))
    w_own = w_qkv[0]
    w_oth = to_partner(w_own)
    o_own = w_out[0]
    o_oth = to_partner(o_own)
    x_oth = got[:HALF]
    g_own = norm_gain.astype(f32)
    g_oth = got[HALF:].astype(f32)
    cache_rows = cache[0].reshape(TICKS, HALF * CACHE, -1)

    batches = jnp.maximum(section - jnp.arange(TICKS, dtype=jnp.int32), 0)
    lens = lax.dynamic_slice_in_dim(lengths, side * HALF, HALF, 1)[batches]
    hi = lens + jnp.arange(HALF, dtype=jnp.int32)[None, :] * CACHE
    hi = jnp.tile(hi, (1, RATIO))[:, :, None]

    gains = jnp.concatenate([g_own.reshape(shards, block), g_oth.reshape(shards, block)], axis=1)
    inverse_gains = 1.0 / gains
    my_gain = lax.dynamic_slice_in_dim(gains, column, 1, 0)
    x_shard = jnp.concatenate(
        [
            lax.dynamic_slice_in_dim(mine, column * block, block, 1),
            lax.dynamic_slice_in_dim(x_oth, column * block, block, 1),
        ],
        axis=1,
    ).astype(f32)

    shared = (hi, w_own, w_oth, o_own, o_oth, cache_rows)
    latest = None
    finals = []
    for tick in range(TICKS):
        if tick == 0:
            terms = run_kernel(
                functools.partial(first_kernel, tick),
                shards, block, mine, x_oth, g_own, g_oth, *shared,
            )
        else:
            scaled = gather((x_shard * my_gain).astype(bf16))
            terms = run_kernel(
                functools.partial(later_kernel, tick),
                shards, block, scaled, inverse_gains, *shared,
            )
        produced = x_shard + jnp.sum(exchange(terms).astype(f32), axis=0)
        latest = produced if tick == 0 else jnp.where(section >= tick, produced, latest)
        rounded = produced.astype(bf16)
        finals.append(rounded)
        if tick + 1 < TICKS:
            x_shard = to_next(rounded).astype(f32)

    def whole_rows(value):
        other = to_partner(value)
        other = jnp.concatenate([other[..., block:], other[..., :block]], axis=-1)
        first = jnp.where(side == 0, value, other)
        second = jnp.where(side == 0, other, value)
        return jnp.concatenate([first, second], axis=-2)

    last_rows = whole_rows(latest.astype(bf16))
    leaving = gather(last_rows[:, :block])
    leaving = leaving.transpose(1, 0, 2).reshape(B, width).astype(f32)

    early = whole_rows(from_last(jnp.stack(finals[:-1]), position))
    final = from_last(last_rows, position)
    talk_rows = jnp.concatenate([early, final[None]], axis=0).astype(f32).reshape(TICKS * B, -1)
    squares = jnp.sum(talk_rows * talk_rows, axis=-1)
    ordered_gain = jnp.where(side == 0, talk_gain, talk_gain[::-1]).astype(f32).reshape(-1)
    ordered_adapt = jnp.where(side == 0, w_adapt, w_adapt[::-1]).reshape(2 * block, -1)
    adapted = jnp.dot(
        (talk_rows * ordered_gain).astype(bf16), ordered_adapt, preferred_element_type=f32
    )
    entries = codebooks.shape[1]
    local_ids = codes.reshape(TICKS * B, NQ) - column * entries
    one_hot = local_ids[:, :, None] == jnp.arange(entries, dtype=jnp.int32)
    one_hot = one_hot.astype(bf16).reshape(TICKS * B, NQ * entries)
    embedded = jnp.dot(
        one_hot, codebooks.reshape(NQ * entries, -1), preferred_element_type=f32
    )
    squares_high = squares.astype(bf16)
    squares_low = (squares - squares_high.astype(f32)).astype(bf16)
    columns = adapted.shape[1]
    payload = jnp.concatenate(
        [
            adapted.astype(bf16),
            embedded.astype(bf16),
            squares_high[:, None],
            squares_low[:, None],
            jnp.zeros((TICKS * B, 126 - 2 * columns), bf16),
        ],
        axis=1,
    )
    sums = jnp.sum(gather(payload).astype(f32), axis=0)
    talk_squares = sums[:, 2 * columns : 2 * columns + 1] + sums[:, 2 * columns + 1 : 2 * columns + 2]
    talk_rms = lax.rsqrt(talk_squares / D + epsilon)
    talk = sums[:, :columns] * talk_rms + sums[:, columns : 2 * columns]
    return (leaving[None], talk.reshape(TICKS, B, columns))


def solution(mesh):
    placed = (
        P("section", None, None),
        P("section", None),
        P("section", None, "tp"),
        P("section", "tp", None),
        P("section", None, None, None, "tp"),
        P(),
        P(None, "tp"),
        P(None, "tp", "section"),
        P(None, "tp", "section"),
        P(),
    )
    return jax.shard_map(
        body,
        mesh=mesh,
        in_specs=placed,
        out_specs=(P("section", None, None), P(None, None, "section")),
        check_vma=False,
    )
```

```python
import functools

import jax
import jax.numpy as jnp
from jax import lax
from jax.experimental import pallas as pl
from jax.experimental.pallas import tpu as pltpu
from jax.sharding import PartitionSpec as P

D = 4096
H = 32
KVH = 8
HD = 64
NQ = 4
TICKS = 4
B = 96
CACHE = 16
HALF = B // 2
RATIO = H // KVH
EARLY = TICKS - 1
LANES = 128
FIRST = 24

epsilon = 1e-05
f32 = jnp.float32
bf16 = jnp.bfloat16
i32 = jnp.int32
CONTRACT_LAST = (((1,), (1,)), ((), ()))


def last_visible(tick, place_ref, lengths_ref):
    side, section = place_ref[0], place_ref[1]
    lens = lengths_ref[pl.ds(jnp.maximum(section - tick, 0), 1), :]
    row = lax.broadcasted_iota(i32, (HALF, B), 0)
    lane = lax.broadcasted_iota(i32, (HALF, B), 1)
    lens = jnp.where(lane == row + side * HALF, lens, 0)
    lens = jnp.sum(lens, axis=1, keepdims=True)
    ends = lens + lax.broadcasted_iota(i32, (HALF, 1), 0) * CACHE
    return jnp.concatenate([ends] * RATIO, axis=0)


def attention_terms(proj, ends, o_own, o_oth, pairs_ref, out_ref):
    shards, block = out_ref.shape[0], out_ref.shape[2] // 2
    stacked = jnp.concatenate([proj[:, r * HD : (r + 1) * HD] for r in range(RATIO)], axis=0)
    queries = (stacked.astype(bf16).astype(f32) * (HD**-0.5)).astype(bf16)
    queries = jnp.concatenate([queries, jnp.zeros_like(queries)], axis=1)
    pair_new = proj[:, RATIO * HD :].astype(bf16)
    pairs = pairs_ref[...]
    scores = lax.dot_general(queries, pairs, CONTRACT_LAST, preferred_element_type=f32)
    own_scores = lax.dot_general(queries, pair_new, CONTRACT_LAST, preferred_element_type=f32)
    rows = RATIO * HALF
    stream = lax.rem(lax.broadcasted_iota(i32, (rows, 1), 0), HALF)
    place = lax.broadcasted_iota(i32, (rows, HALF * CACHE), 1)
    visible = jnp.logical_and(place >= stream * CACHE, place < ends)
    scores = jnp.where(visible, scores, -jnp.inf)
    own_place = lax.broadcasted_iota(i32, (rows, HALF), 1)
    own_scores = jnp.where(own_place == stream, own_scores, -jnp.inf)
    row_max = jnp.maximum(
        jnp.max(scores, axis=-1, keepdims=True), jnp.max(own_scores, axis=-1, keepdims=True)
    )
    weights = jnp.exp(scores - row_max)
    own_weights = jnp.exp(own_scores - row_max)
    total = jnp.sum(weights, axis=-1, keepdims=True) + jnp.sum(own_weights, axis=-1, keepdims=True)
    share = 1.0 / total
    mixed = jnp.dot((weights * share).astype(bf16), pairs, preferred_element_type=f32)
    mixed = mixed + jnp.dot(
        (own_weights * share).astype(bf16), pair_new, preferred_element_type=f32
    )
    mixed = mixed[:, HD:].astype(bf16)
    heads = jnp.concatenate([mixed[r * HALF : (r + 1) * HALF] for r in range(RATIO)], axis=1)
    for j in range(shards):
        span = slice(j * block, (j + 1) * block)
        own = jnp.dot(heads, o_own[:, span], preferred_element_type=f32)
        oth = jnp.dot(heads, o_oth[:, span], preferred_element_type=f32)
        out_ref[j, :, :block] = own.astype(bf16)
        out_ref[j, :, block:] = oth.astype(bf16)


def first_kernel(place_ref, *refs):
    count = (len(refs) - 3) // 2
    sources, (out_ref, shard_ref), held = refs[:count], refs[count : count + 2], refs[count + 2 : -1]
    semaphores = refs[-1]
    copies = [
        pltpu.make_async_copy(source, target, semaphores.at[i])
        for i, (source, target) in enumerate(zip(sources, held))
    ]
    for copy in copies:
        copy.start()
    rows_own, rows_oth, g_own, g_oth, lengths_ref, w_own, w_oth, o_own, o_oth = held[:9]
    side, column = place_ref[0], place_ref[2]
    block = shard_ref.shape[1] // 2
    mine = pl.ds(pl.multiple_of(side * HALF, HALF), HALF)
    for copy in copies[:5]:
        copy.wait()
    own = rows_own[mine, :].astype(f32)
    oth = rows_oth[mine, :].astype(f32)
    squares = jnp.sum(own * own + oth * oth, axis=-1, keepdims=True)
    scaled_own = (own * g_own[...].astype(f32)).astype(bf16)
    scaled_oth = (oth * g_oth[...].astype(f32)).astype(bf16)
    part = pl.ds(pl.multiple_of(column * block, block), block)
    shard_ref[:, :block] = rows_own[mine, part]
    shard_ref[:, block:] = rows_oth[mine, part]
    ends = last_visible(0, place_ref, lengths_ref)
    copies[5].wait()
    proj = jnp.dot(scaled_own, w_own[...], preferred_element_type=f32)
    copies[6].wait()
    proj = proj + jnp.dot(scaled_oth, w_oth[...], preferred_element_type=f32)
    proj = proj * lax.rsqrt(squares / D + epsilon)
    for copy in copies[7:]:
        copy.wait()
    attention_terms(proj, ends, o_own, o_oth, held[9].at[0], out_ref)


def later_kernel(
    tick, place_ref, lengths_ref, g_own, g_oth, w_own, w_oth, o_own, o_oth, cache_ref, x_ref,
    out_ref, inverse_ref,
):
    shards, block = x_ref.shape[0], x_ref.shape[2] // 2
    squares = jnp.zeros(x_ref.shape[1:], f32)
    proj = jnp.zeros((HALF, w_own.shape[1]), f32)
    for j in range(shards):
        span = slice(j * block, (j + 1) * block)
        rows = x_ref[j].astype(f32)
        squares = squares + rows * rows
        own = (rows[:, :block] * g_own[:, span].astype(f32)).astype(bf16)
        oth = (rows[:, block:] * g_oth[:, span].astype(f32)).astype(bf16)
        proj = proj + jnp.dot(own, w_own[span, :], preferred_element_type=f32)
        proj = proj + jnp.dot(oth, w_oth[span, :], preferred_element_type=f32)
    inverse_rms = lax.rsqrt(jnp.sum(squares, axis=-1, keepdims=True) / D + epsilon)
    inverse_ref[...] = jnp.broadcast_to(inverse_rms, inverse_ref.shape)
    proj = proj * inverse_rms
    ends = last_visible(tick, place_ref, lengths_ref)
    attention_terms(proj, ends, o_own, o_oth, cache_ref.at[tick], out_ref)


def sum_kernel(tick, place_ref, got_ref, shard_ref, inverse_ref, out_ref):
    section = place_ref[1]
    shard = shard_ref[...].astype(f32)
    total = shard
    for j in range(got_ref.shape[0]):
        total = total + got_ref[j].astype(f32)
    if tick:
        passed = shard * jnp.where(section == 0, inverse_ref[:, :1], 1.0)
        total = jnp.where(section >= tick, total, passed)
    out_ref[...] = total.astype(bf16)


def latest_kernel(place_ref, last_ref, early_0, early_1, early_2, out_ref):
    section = place_ref[1]
    latest = last_ref[...].astype(f32)
    for tick, early in ((2, early_2), (1, early_1), (0, early_0)):
        latest = jnp.where(section <= tick, early[...].astype(f32), latest)
    out_ref[...] = latest.astype(bf16)


def holder_of(tick):
    return EARLY if tick == EARLY else EARLY - 1 - tick


def talk_kernel(
    place_ref, own_ref, other_ref, latest_own, latest_oth, talk_gain, adapt_ref, books_ref, codes_ref,
    out_ref,
):
    side, column = place_ref[0], place_ref[2]
    block = own_ref.shape[2] // 2
    columns = adapt_ref.shape[1]
    entries = books_ref.shape[2]
    gains = talk_gain[...].astype(f32)

    def whole(tick):
        own = own_ref[holder_of(tick)].astype(f32)
        other = other_ref[holder_of(tick)].astype(f32)
        first = jnp.where(side == 0, own, other)
        second = jnp.where(side == 0, other, own)
        return (
            jnp.concatenate([first[:, :block], second[:, block:]], axis=0),
            jnp.concatenate([first[:, block:], second[:, :block]], axis=0),
        )

    def embedded(tick):
        total = jnp.zeros((columns, B), f32)
        for q in range(NQ):
            ids = codes_ref[tick, q : q + 1, :] - column * entries
            hot = lax.broadcasted_iota(i32, (entries, B), 0) == ids
            hot = jnp.where(hot, 1.0, 0.0).astype(bf16)
            total = total + jnp.dot(books_ref[q], hot, preferred_element_type=f32)
        return total

    def adapted(low, high):
        return lax.dot_general(
            adapt_ref[0], low.astype(bf16), CONTRACT_LAST, preferred_element_type=f32
        ) + lax.dot_general(
            adapt_ref[1], high.astype(bf16), CONTRACT_LAST, preferred_element_type=f32
        )

    out_ref[: (TICKS + 1) * columns + 16] = jnp.zeros(((TICKS + 1) * columns + 16, LANES), bf16)
    for tick in range(TICKS):
        low, high = whole(tick)
        rows = adapted(low * gains[0:1], high * gains[1:2])
        base = tick * columns
        if tick < EARLY:
            rows = rows + embedded(tick)
        else:
            out_ref[base + columns : base + 2 * columns, :B] = embedded(tick).astype(bf16)
        out_ref[base : base + columns, :B] = rows.astype(bf16)
    squares = jnp.sum(low * low + high * high, axis=1, keepdims=True)
    diagonal = lax.broadcasted_iota(i32, (B, B), 0) == lax.broadcasted_iota(i32, (B, B), 1)
    squares = jnp.sum(jnp.where(diagonal, squares, 0.0), axis=0, keepdims=True)
    upper = squares.astype(bf16).astype(f32)
    tail_row = lax.broadcasted_iota(i32, (16, B), 0)
    tail = jnp.where(tail_row == 0, upper, jnp.where(tail_row == 1, squares - upper, 0.0))
    base = (TICKS + 1) * columns + 16
    out_ref[base - 16 : base, :B] = tail.astype(bf16)
    own = latest_own[:, :block].astype(f32)
    oth = latest_oth[:, block:].astype(f32)
    first = jnp.where(side == 0, own, oth).astype(bf16)
    second = jnp.where(side == 0, oth, own).astype(bf16)
    for i in range(block // LANES):
        span = slice(i * LANES, (i + 1) * LANES)
        out_ref[base + i * B : base + i * B + HALF, :] = first[:, span]
        out_ref[base + i * B + HALF : base + (i + 1) * B, :] = second[:, span]


def finish_kernel(got_ref, out_ref, leaving_ref):
    columns = out_ref.shape[1]
    end = (TICKS + 1) * columns + 16
    pieces = (got_ref.shape[1] - end) // B
    total = got_ref[0, :end].astype(f32)
    for j in range(1, got_ref.shape[0]):
        total = total + got_ref[j, :end].astype(f32)
    for j in range(got_ref.shape[0]):
        for i in range(pieces):
            lane = (j * pieces + i) * LANES
            rows = got_ref[j, end + i * B : end + (i + 1) * B, :]
            leaving_ref[:, lane : lane + LANES] = rows.astype(f32)
    for tick in range(EARLY):
        out_ref[tick] = total[tick * columns : (tick + 1) * columns, :B]
    base, at = EARLY * columns, (TICKS + 1) * columns
    squares = total[at : at + 1, :] + total[at + 1 : at + 2, :]
    rows = total[base : base + columns] * lax.rsqrt(squares / D + epsilon)
    rows = rows + total[base + columns : base + 2 * columns]
    out_ref[EARLY] = rows[:, :B]


def run(kernel, outs, *operands, scalars=True, limit=16):
    specs = [pl.BlockSpec(memory_space=pltpu.VMEM)] * len(operands)
    if scalars:
        specs[0] = pl.BlockSpec(memory_space=pltpu.SMEM)
    out_specs = jax.tree.map(lambda _: pl.BlockSpec(memory_space=pltpu.VMEM), outs)
    return pl.pallas_call(
        kernel,
        out_shape=outs,
        in_specs=specs,
        out_specs=out_specs,
        compiler_params=pltpu.CompilerParams(vmem_limit_bytes=limit * 2**20),
    )(*operands)


def shaped(*shape, dtype=bf16):
    return jax.ShapeDtypeStruct(shape, dtype)


SECTION = ("line", "place", "core")
LINES, PLACES = 8, 4
LINE = 2 * PLACES


def to_partner(value):
    return lax.ppermute(value, "core", [(0, 1), (1, 0)])


def to_next(value):
    count = LINES * LINE
    return lax.ppermute(value, SECTION, [(i, (i + 2) % count) for i in range(count)])


def exchange(blocks, axis="tp"):
    return lax.all_to_all(blocks, axis, 0, 0, tiled=True)


def replicate(block, count):
    return jnp.broadcast_to(block[None], (count,) + block.shape)


def across_lines(value, holds):
    home = [LINES - 1 if place == EARLY else 0 for place in range(PLACES)]
    steps = sorted(range(1, LINES), key=lambda d: -min(d, LINES - d))
    result = jnp.where(holds, value, jnp.zeros_like(value))
    for d in steps:
        pairs = [
            (home[i // 2] * LINE + i, (home[i // 2] + d) % LINES * LINE + i) for i in range(LINE)
        ]
        result = result + lax.ppermute(value, SECTION, pairs)
    return result


def body(arriving, norm_gain, w_qkv, w_out, cache, lengths, talk_gain, w_adapt, codebooks, codes):
    position = lax.axis_index(SECTION)
    column = lax.axis_index("tp")
    shards = lax.axis_size("tp")
    section = position // 2
    width = arriving.shape[2]
    block = width // shards
    columns = w_adapt.shape[2]
    place = jnp.stack([lax.rem(position, 2), section, column]).astype(i32)

    w_own, o_own, rows_own = w_qkv[0], w_out[0], arriving[0]
    rows_oth = to_partner(rows_own)
    w_oth = to_partner(w_own)
    g_oth = to_partner(norm_gain)
    o_oth = to_partner(o_own)
    cache_rows = cache[0].reshape(TICKS, HALF * CACHE, -1)
    blocks = shaped(shards, HALF, 2 * block)
    piece = shaped(HALF, 2 * block)

    rows_own, norm_gain, lengths, w_own, o_own, cache_rows = (
        pltpu.with_memory_space_constraint(v, pltpu.HBM)
        for v in (rows_own, norm_gain, lengths, w_own, o_own, cache_rows)
    )
    held = [rows_own, rows_oth, norm_gain, g_oth, lengths, w_own, w_oth, o_own, o_oth, cache_rows]
    there = pl.BlockSpec(memory_space=pltpu.HBM)
    here = pl.BlockSpec(memory_space=pltpu.VMEM)
    terms, shard, _, _, *held = pl.pallas_call(
        first_kernel,
        out_shape=(blocks, piece, *(shaped(*v.shape, dtype=v.dtype) for v in held)),
        in_specs=[pl.BlockSpec(memory_space=pltpu.SMEM)] + [there] * len(held),
        out_specs=(here,) * (len(held) + 2),
        scratch_shapes=[pltpu.SemaphoreType.DMA((len(held),))],
        compiler_params=pltpu.CompilerParams(vmem_limit_bytes=FIRST * 2**20),
    )(place, *held)
    g_own, g_oth, lengths, *weights = held
    shared = (place, lengths, g_own, g_oth, *weights)
    finals = []
    inverse = jnp.zeros((HALF, LANES), f32)
    for tick in range(EARLY):
        got = exchange(terms)
        finals.append(run(functools.partial(sum_kernel, tick), piece, place, got, shard, inverse))
        shard = to_next(finals[-1])
        rows = exchange(replicate(shard, shards))
        terms, inverse = run(
            functools.partial(later_kernel, tick + 1),
            (blocks, shaped(HALF, LANES, dtype=f32)),
            *shared, rows,
        )
    got = exchange(terms)
    held_rows = run(functools.partial(sum_kernel, EARLY), piece, place, got, shard, inverse)

    holds = jnp.logical_or(section < EARLY, section == LINES * PLACES - 1)
    talk_rows = across_lines(held_rows, holds)
    latest = run(latest_kernel, piece, place, held_rows, *finals)
    latest_oth = to_partner(latest)
    talk_rows, latest_oth = lax.optimization_barrier((talk_rows, latest_oth))
    talk_rows = exchange(replicate(talk_rows, PLACES), "place")
    payload = run(
        talk_kernel,
        shaped((TICKS + 1) * columns + 16 + B * block // LANES, LANES),
        place, talk_rows, to_partner(talk_rows), latest, latest_oth, talk_gain,
        w_adapt.transpose(0, 2, 1), codebooks.transpose(0, 2, 1), codes.transpose(0, 2, 1),
    )
    sums = exchange(replicate(payload, shards))
    talk, leaving = run(
        finish_kernel,
        (shaped(TICKS, columns, B, dtype=f32), shaped(B, width, dtype=f32)),
        sums,
        scalars=False,
    )
    return (leaving[None], talk.transpose(0, 2, 1))


def solution(mesh):
    devices = mesh.devices
    grid = jax.sharding.Mesh(
        devices.reshape(LINES, PLACES, 2, devices.shape[1]), SECTION + ("tp",)
    )
    placed = (
        P(SECTION, None, None),
        P(SECTION, None),
        P(SECTION, None, "tp"),
        P(SECTION, "tp", None),
        P(SECTION, None, None, None, "tp"),
        P(),
        P(None, "tp"),
        P(None, "tp", SECTION),
        P(None, "tp", SECTION),
        P(),
    )
    return jax.shard_map(
        body,
        mesh=grid,
        in_specs=placed,
        out_specs=(P(SECTION, None, None), P(None, None, SECTION)),
        check_vma=False,
    )
```

```python
import functools

import jax
import jax.numpy as jnp
from jax import lax
from jax.experimental import pallas as pl
from jax.experimental.pallas import tpu as pltpu
from jax.sharding import PartitionSpec as P

D = 4096
H = 32
KVH = 8
HD = 64
NQ = 4
TICKS = 4
B = 96
CACHE = 16
HALF = B // 2
RATIO = H // KVH
EARLY = TICKS - 1
LANES = 128
FIRST = 24

epsilon = 1e-05
f32 = jnp.float32
bf16 = jnp.bfloat16
i32 = jnp.int32
CONTRACT_LAST = (((1,), (1,)), ((), ()))


def last_visible(tick, place_ref, lengths_ref):
    side, section = place_ref[0], place_ref[1]
    lens = lengths_ref[pl.ds(jnp.maximum(section - tick, 0), 1), :]
    row = lax.broadcasted_iota(i32, (HALF, B), 0)
    lane = lax.broadcasted_iota(i32, (HALF, B), 1)
    lens = jnp.where(lane == row + side * HALF, lens, 0)
    lens = jnp.sum(lens, axis=1, keepdims=True)
    ends = lens + lax.broadcasted_iota(i32, (HALF, 1), 0) * CACHE
    return jnp.concatenate([ends] * RATIO, axis=0)


def attention_terms(proj, ends, o_own, o_oth, pairs_ref, out_ref):
    shards, block = out_ref.shape[0], out_ref.shape[2] // 2
    stacked = jnp.concatenate([proj[:, r * HD : (r + 1) * HD] for r in range(RATIO)], axis=0)
    queries = (stacked.astype(bf16).astype(f32) * (HD**-0.5)).astype(bf16)
    queries = jnp.concatenate([queries, jnp.zeros_like(queries)], axis=1)
    pair_new = proj[:, RATIO * HD :].astype(bf16)
    pairs = pairs_ref[...]
    scores = lax.dot_general(queries, pairs, CONTRACT_LAST, preferred_element_type=f32)
    own_scores = lax.dot_general(queries, pair_new, CONTRACT_LAST, preferred_element_type=f32)
    rows = RATIO * HALF
    stream = lax.rem(lax.broadcasted_iota(i32, (rows, 1), 0), HALF)
    place = lax.broadcasted_iota(i32, (rows, HALF * CACHE), 1)
    visible = jnp.logical_and(place >= stream * CACHE, place < ends)
    scores = jnp.where(visible, scores, -jnp.inf)
    own_place = lax.broadcasted_iota(i32, (rows, HALF), 1)
    own_scores = jnp.where(own_place == stream, own_scores, -jnp.inf)
    row_max = jnp.maximum(
        jnp.max(scores, axis=-1, keepdims=True), jnp.max(own_scores, axis=-1, keepdims=True)
    )
    weights = jnp.exp(scores - row_max)
    own_weights = jnp.exp(own_scores - row_max)
    total = jnp.sum(weights, axis=-1, keepdims=True) + jnp.sum(own_weights, axis=-1, keepdims=True)
    share = 1.0 / total
    mixed = jnp.dot((weights * share).astype(bf16), pairs, preferred_element_type=f32)
    mixed = mixed + jnp.dot(
        (own_weights * share).astype(bf16), pair_new, preferred_element_type=f32
    )
    mixed = mixed[:, HD:].astype(bf16)
    heads = jnp.concatenate([mixed[r * HALF : (r + 1) * HALF] for r in range(RATIO)], axis=1)
    for j in range(shards):
        span = slice(j * block, (j + 1) * block)
        own = jnp.dot(heads, o_own[:, span], preferred_element_type=f32)
        oth = jnp.dot(heads, o_oth[:, span], preferred_element_type=f32)
        out_ref[j, :, :block] = own.astype(bf16)
        out_ref[j, :, block:] = oth.astype(bf16)


def pack_kernel(rows_src, gain_src, adapt_src, books_src, out_ref, gain_ref, semaphores):
    columns, entries = adapt_src.shape[1:]
    tables = [adapt_src.at[i] for i in range(adapt_src.shape[0])]
    tables += [books_src.at[q] for q in range(NQ)]
    below = pl.ds(B, columns)
    copies = [pltpu.make_async_copy(gain_src, gain_ref, semaphores.at[0])]
    copies += [pltpu.make_async_copy(rows_src, out_ref.at[:B], semaphores.at[1])]
    for i, source in enumerate(tables):
        target = out_ref.at[below, pl.ds(i * entries, entries)]
        copies += [pltpu.make_async_copy(source, target, semaphores.at[2 + i])]
    for copy in copies:
        copy.start()
    start = len(tables) * entries
    free = out_ref.shape[1] - start
    copies[0].wait()
    gain = gain_ref[...].astype(f32)
    pieces = [gain[:, j : j + free] for j in range(0, gain.shape[1], free)]
    pieces += [jnp.zeros((columns - len(pieces), free), f32)]
    out_ref[B:, start:] = jnp.concatenate(pieces, axis=0).astype(bf16)
    for copy in copies[1:]:
        copy.wait()


def unpacked_gain(packed_ref):
    width = packed_ref.shape[1]
    start = (2 + NQ) * (width // 8)
    held = packed_ref[B:, start:].astype(f32)
    count = width // (width - start)
    return jnp.concatenate([held[j : j + 1] for j in range(count)], axis=1)


def first_kernel(
    place_ref, packed_own, packed_oth, w_oth, o_oth, lens_src, w_src, o_src, cache_src,
    out_ref, shard_ref, g_own_ref, g_oth_ref, lengths_ref, w_own, o_own, cache_ref, semaphores,
):
    sources = (lens_src, w_src, o_src, cache_src)
    held = (lengths_ref, w_own, o_own, cache_ref)
    copies = [
        pltpu.make_async_copy(source, target, semaphores.at[i])
        for i, (source, target) in enumerate(zip(sources, held))
    ]
    for copy in copies:
        copy.start()
    side, column = place_ref[0], place_ref[2]
    block = shard_ref.shape[1] // 2
    mine = pl.ds(pl.multiple_of(side * HALF, HALF), HALF)
    own = packed_own[mine, :].astype(f32)
    oth = packed_oth[mine, :].astype(f32)
    squares = jnp.sum(own * own + oth * oth, axis=-1, keepdims=True)
    gains = [unpacked_gain(packed_own), unpacked_gain(packed_oth)]
    g_own_ref[...], g_oth_ref[...] = gains
    scaled_own = (own * gains[0]).astype(bf16)
    scaled_oth = (oth * gains[1]).astype(bf16)
    part = pl.ds(pl.multiple_of(column * block, block), block)
    shard_ref[:, :block] = packed_own[mine, part]
    shard_ref[:, block:] = packed_oth[mine, part]
    copies[0].wait()
    ends = last_visible(0, place_ref, lengths_ref)
    proj = jnp.dot(scaled_oth, w_oth[...], preferred_element_type=f32)
    copies[1].wait()
    proj = proj + jnp.dot(scaled_own, w_own[...], preferred_element_type=f32)
    proj = proj * lax.rsqrt(squares / D + epsilon)
    for copy in copies[2:]:
        copy.wait()
    attention_terms(proj, ends, o_own, o_oth, cache_ref.at[0], out_ref)


def later_kernel(
    tick, place_ref, lengths_ref, g_own, g_oth, w_own, w_oth, o_own, o_oth, cache_ref, x_ref,
    out_ref, inverse_ref,
):
    shards, block = x_ref.shape[0], x_ref.shape[2] // 2
    squares = jnp.zeros(x_ref.shape[1:], f32)
    proj = jnp.zeros((HALF, w_own.shape[1]), f32)
    for j in range(shards):
        span = slice(j * block, (j + 1) * block)
        rows = x_ref[j].astype(f32)
        squares = squares + rows * rows
        own = (rows[:, :block] * g_own[:, span]).astype(bf16)
        oth = (rows[:, block:] * g_oth[:, span]).astype(bf16)
        proj = proj + jnp.dot(own, w_own[span, :], preferred_element_type=f32)
        proj = proj + jnp.dot(oth, w_oth[span, :], preferred_element_type=f32)
    inverse_rms = lax.rsqrt(jnp.sum(squares, axis=-1, keepdims=True) / D + epsilon)
    inverse_ref[...] = jnp.broadcast_to(inverse_rms, inverse_ref.shape)
    proj = proj * inverse_rms
    ends = last_visible(tick, place_ref, lengths_ref)
    attention_terms(proj, ends, o_own, o_oth, cache_ref.at[tick], out_ref)


def sum_kernel(tick, place_ref, got_ref, shard_ref, inverse_ref, out_ref):
    section = place_ref[1]
    shard = shard_ref[...].astype(f32)
    total = shard
    for j in range(got_ref.shape[0]):
        total = total + got_ref[j].astype(f32)
    if tick:
        passed = shard * jnp.where(section == 0, inverse_ref[:, :1], 1.0)
        total = jnp.where(section >= tick, total, passed)
    out_ref[...] = total.astype(bf16)


def last_sum_kernel(
    place_ref, got_ref, shard_ref, inverse_ref, early_0, early_1, early_2, out_ref, latest_ref
):
    sum_kernel(EARLY, place_ref, got_ref, shard_ref, inverse_ref, out_ref)
    section = place_ref[1]
    latest = out_ref[...].astype(f32)
    for tick, early in ((2, early_2), (1, early_1), (0, early_0)):
        latest = jnp.where(section <= tick, early[...].astype(f32), latest)
    latest_ref[...] = latest.astype(bf16)


def holder_of(tick):
    return EARLY if tick == EARLY else EARLY - 1 - tick


def talk_kernel(
    place_ref, rows_ref, latest_ref, talk_gain, packed_own, packed_oth, codes_ref, out_ref
):
    side, column = place_ref[0], place_ref[2]
    block = rows_ref.shape[2] // 2
    columns, entries = packed_own.shape[0] - B, packed_own.shape[1] // 8
    first = side == 0
    gains = talk_gain[...].astype(f32)

    def halves(rows):
        own, oth = rows[:, :block].astype(f32), rows[:, block:].astype(f32)
        return jnp.where(first, own, oth), jnp.where(first, oth, own)

    def table(i):
        span = slice(i * entries, (i + 1) * entries)
        own, oth = packed_own[B:, span].astype(f32), packed_oth[B:, span].astype(f32)
        both = [jnp.where(first, own, oth), jnp.where(first, oth, own)]
        return jnp.concatenate(both, axis=0).astype(bf16)

    def beside(terms):
        return jnp.concatenate([terms[:columns], terms[columns:]], axis=1)

    def embedded(tick):
        total = jnp.zeros((2 * columns, B), f32)
        for q in range(NQ):
            ids = codes_ref[tick, q : q + 1, :] - column * entries
            hot = lax.broadcasted_iota(i32, (entries, B), 0) == ids
            hot = jnp.where(hot, 1.0, 0.0).astype(bf16)
            total = total + jnp.dot(books[q], hot, preferred_element_type=f32)
        return beside(jnp.where(first, total[:, :HALF], total[:, HALF:]))

    adapt = [table(0), table(1)]
    books = [table(2 + q) for q in range(NQ)]
    pieces = []
    for tick in range(TICKS):
        low, high = halves(rows_ref[holder_of(tick)])
        terms = jnp.zeros((2 * columns, HALF), f32)
        for i, part in enumerate((low, high)):
            scaled = (part * gains[i : i + 1]).astype(bf16)
            terms = terms + lax.dot_general(
                adapt[i], scaled, CONTRACT_LAST, preferred_element_type=f32
            )
        terms = beside(terms)
        pieces += [terms + embedded(tick)] if tick < EARLY else [terms, embedded(tick)]
    squares = jnp.sum(low * low + high * high, axis=1, keepdims=True)
    squares = jnp.concatenate([squares, squares], axis=0)
    upper = squares.astype(bf16).astype(f32)
    grid = jnp.concatenate(pieces, axis=0)
    grid = jnp.concatenate([grid, jnp.zeros((grid.shape[0], LANES - B), f32)], axis=1)
    grid = jnp.concatenate([grid, jnp.zeros((2 * LANES - grid.shape[0], LANES), f32)], axis=0)
    grid = grid.T[:B]
    lane = lax.broadcasted_iota(i32, grid.shape, 1)
    grid = jnp.where(lane == (TICKS + 1) * columns, upper, grid)
    grid = jnp.where(lane == (TICKS + 1) * columns + 1, squares - upper, grid)
    for c, part in enumerate(halves(latest_ref[...])):
        out_ref[c, :HALF] = grid[c * HALF : (c + 1) * HALF].astype(bf16)
        out_ref[c, HALF:] = part.astype(bf16)


def finish_kernel(got_ref, out_ref, leaving_ref):
    columns, block = out_ref.shape[1], got_ref.shape[2]
    shards = got_ref.shape[0] // 2
    tables = []
    for c in range(2):
        table = got_ref[c * shards, :HALF].astype(f32)
        for j in range(1, shards):
            table = table + got_ref[c * shards + j, :HALF].astype(f32)
        tables.append(table)
        for j in range(shards):
            rows = got_ref[c * shards + j, HALF:].astype(f32)
            leaving_ref[c * HALF : (c + 1) * HALF, j * block : (j + 1) * block] = rows
    table = jnp.concatenate(tables, axis=0)
    table = jnp.concatenate([table, jnp.zeros((LANES - B, block), f32)], axis=0).T
    for tick in range(EARLY):
        out_ref[tick] = table[tick * columns : (tick + 1) * columns, :B]
    base, at = EARLY * columns, (TICKS + 1) * columns
    squares = table[at : at + 1, :] + table[at + 1 : at + 2, :]
    rows = table[base : base + columns] * lax.rsqrt(squares / D + epsilon)
    rows = rows + table[base + columns : base + 2 * columns]
    out_ref[EARLY] = rows[:, :B]


def run(kernel, outs, *operands, scalars=True, limit=16):
    specs = [pl.BlockSpec(memory_space=pltpu.VMEM)] * len(operands)
    if scalars:
        specs[0] = pl.BlockSpec(memory_space=pltpu.SMEM)
    out_specs = jax.tree.map(lambda _: pl.BlockSpec(memory_space=pltpu.VMEM), outs)
    return pl.pallas_call(
        kernel,
        out_shape=outs,
        in_specs=specs,
        out_specs=out_specs,
        compiler_params=pltpu.CompilerParams(vmem_limit_bytes=limit * 2**20),
    )(*operands)


def shaped(*shape, dtype=bf16):
    return jax.ShapeDtypeStruct(shape, dtype)


SECTION = ("line", "place", "core")
LINES, PLACES = 8, 4
LINE = 2 * PLACES


def to_partner(value):
    return lax.ppermute(value, "core", [(0, 1), (1, 0)])


def to_next(value):
    count = LINES * LINE
    return lax.ppermute(value, SECTION, [(i, (i + 2) % count) for i in range(count)])


def exchange(blocks, axis="tp"):
    return lax.all_to_all(blocks, axis, 0, 0, tiled=True)


def replicate(block, count):
    return jnp.broadcast_to(block[None], (count,) + block.shape)


def across_lines(value, line):
    home = [LINES - 1 if place == EARLY else 0 for place in range(PLACES)]

    def sent(rows, start, step):
        return lax.ppermute(
            rows,
            SECTION,
            [
                ((home[i // 2] + d) % LINES * LINE + i, (home[i // 2] + d + step) % LINES * LINE + i)
                for d in start
                for i in range(LINE)
            ],
        )

    place = lax.axis_index("place")
    offset = lax.rem(line - jnp.where(place == EARLY, LINES - 1, 0) + LINES, LINES)
    some = jnp.where(offset == 0, value, jnp.zeros_like(value))
    for step in (4, 2, 6):
        some = some + sent(value, (0,), step)
    return some + sent(some, (0, 2, 4, 6), 1)


def body(arriving, norm_gain, w_qkv, w_out, cache, lengths, talk_gain, w_adapt, codebooks, codes):
    position = lax.axis_index(SECTION)
    column = lax.axis_index("tp")
    shards = lax.axis_size("tp")
    section = position // 2
    width = arriving.shape[2]
    block = width // shards
    columns = w_adapt.shape[2]
    place = jnp.stack([lax.rem(position, 2), section, column]).astype(i32)

    w_own, o_own = w_qkv[0], w_out[0]
    w_oth = to_partner(w_own)
    o_oth = to_partner(o_own)
    there = pl.BlockSpec(memory_space=pltpu.HBM)
    here = pl.BlockSpec(memory_space=pltpu.VMEM)
    sources = [arriving[0], norm_gain, w_adapt.transpose(0, 2, 1), codebooks.transpose(0, 2, 1)]
    packed_own = pl.pallas_call(
        pack_kernel,
        out_shape=shaped(B + columns, width),
        in_specs=[there] * len(sources),
        out_specs=here,
        scratch_shapes=[
            pltpu.VMEM(norm_gain.shape, bf16), pltpu.SemaphoreType.DMA((4 + NQ,))
        ],
        compiler_params=pltpu.CompilerParams(vmem_limit_bytes=8 * 2**20),
    )(*(pltpu.with_memory_space_constraint(v, pltpu.HBM) for v in sources))
    packed_oth = to_partner(packed_own)
    cache_rows = cache[0].reshape(TICKS, HALF * CACHE, -1)
    blocks = shaped(shards, HALF, 2 * block)
    piece = shaped(HALF, 2 * block)

    sources = [lengths, w_own, o_own, cache_rows]
    gain = shaped(1, width, dtype=f32)
    held = [gain, gain] + [shaped(*v.shape, dtype=v.dtype) for v in sources]
    terms, shard, g_own, g_oth, lengths, w_own, o_own, cache_rows = pl.pallas_call(
        first_kernel,
        out_shape=(blocks, piece, *held),
        in_specs=[pl.BlockSpec(memory_space=pltpu.SMEM)] + [here] * 4 + [there] * len(sources),
        out_specs=(here,) * (len(held) + 2),
        scratch_shapes=[pltpu.SemaphoreType.DMA((len(sources),))],
        compiler_params=pltpu.CompilerParams(vmem_limit_bytes=FIRST * 2**20),
    )(
        place, packed_own, packed_oth, w_oth, o_oth,
        *(pltpu.with_memory_space_constraint(v, pltpu.HBM) for v in sources),
    )
    shared = (place, lengths, g_own, g_oth, w_own, w_oth, o_own, o_oth, cache_rows)
    finals = []
    inverse = jnp.zeros((HALF, LANES), f32)
    for tick in range(EARLY):
        got = exchange(terms)
        finals.append(run(functools.partial(sum_kernel, tick), piece, place, got, shard, inverse))
        shard = to_next(finals[-1])
        rows = exchange(replicate(shard, shards))
        terms, inverse = run(
            functools.partial(later_kernel, tick + 1),
            (blocks, shaped(HALF, LANES, dtype=f32)),
            *shared, rows,
        )
    got = exchange(terms)
    held_rows, latest = run(
        last_sum_kernel, (piece, piece), place, got, shard, inverse, *finals
    )

    talk_rows = across_lines(held_rows, lax.axis_index("line"))
    talk_rows = exchange(replicate(talk_rows, PLACES), "place")
    payload = run(
        talk_kernel,
        shaped(2, B, block),
        place, talk_rows, latest, talk_gain, packed_own, packed_oth, codes.transpose(0, 2, 1),
    )
    payload = jnp.broadcast_to(payload[:, None], (2, shards, B, block))
    sums = exchange(payload.reshape(2 * shards, B, block), ("core", "tp"))
    talk, leaving = run(
        finish_kernel,
        (shaped(TICKS, columns, B, dtype=f32), shaped(B, width, dtype=f32)),
        sums,
        scalars=False,
    )
    return (leaving[None], talk.transpose(0, 2, 1))


def solution(mesh):
    devices = mesh.devices
    grid = jax.sharding.Mesh(
        devices.reshape(LINES, PLACES, 2, devices.shape[1]), SECTION + ("tp",)
    )
    placed = (
        P(SECTION, None, None),
        P(SECTION, None),
        P(SECTION, None, "tp"),
        P(SECTION, "tp", None),
        P(SECTION, None, None, None, "tp"),
        P(),
        P(None, "tp"),
        P(None, "tp", SECTION),
        P(None, "tp", SECTION),
        P(),
    )
    return jax.shard_map(
        body,
        mesh=grid,
        in_specs=placed,
        out_specs=(P(SECTION, None, None), P(None, None, SECTION)),
        check_vma=False,
    )
```

```python
import functools

import jax
import jax.numpy as jnp
from jax import lax
from jax.experimental import pallas as pl
from jax.experimental.pallas import tpu as pltpu
from jax.sharding import PartitionSpec as P

D = 4096
H = 32
KVH = 8
HD = 64
NQ = 4
TICKS = 4
B = 96
CACHE = 16
HALF = B // 2
RATIO = H // KVH
EARLY = TICKS - 1
LANES = 128

epsilon = 1e-05
f32 = jnp.float32
bf16 = jnp.bfloat16
i32 = jnp.int32
CONTRACT_LAST = (((1,), (1,)), ((), ()))


def last_visible(tick, place_ref, lengths_ref):
    side, section = place_ref[0], place_ref[1]
    lens = lengths_ref[pl.ds(jnp.maximum(section - tick, 0), 1), :]
    row = lax.broadcasted_iota(i32, (HALF, B), 0)
    lane = lax.broadcasted_iota(i32, (HALF, B), 1)
    lens = jnp.where(lane == row + side * HALF, lens, 0)
    lens = jnp.sum(lens, axis=1, keepdims=True)
    ends = lens + lax.broadcasted_iota(i32, (HALF, 1), 0) * CACHE
    return jnp.concatenate([ends] * RATIO, axis=0)


def attention_terms(proj, ends, o_own, o_oth, pairs_ref, out_ref):
    shards, block = out_ref.shape[0], out_ref.shape[2] // 2
    stacked = jnp.concatenate([proj[:, r * HD : (r + 1) * HD] for r in range(RATIO)], axis=0)
    queries = (stacked.astype(bf16).astype(f32) * (HD**-0.5)).astype(bf16)
    queries = jnp.concatenate([queries, jnp.zeros_like(queries)], axis=1)
    pair_new = proj[:, RATIO * HD :].astype(bf16)
    pairs = pairs_ref[...]
    scores = lax.dot_general(queries, pairs, CONTRACT_LAST, preferred_element_type=f32)
    own_scores = lax.dot_general(queries, pair_new, CONTRACT_LAST, preferred_element_type=f32)
    rows = RATIO * HALF
    stream = lax.rem(lax.broadcasted_iota(i32, (rows, 1), 0), HALF)
    place = lax.broadcasted_iota(i32, (rows, HALF * CACHE), 1)
    visible = jnp.logical_and(place >= stream * CACHE, place < ends)
    scores = jnp.where(visible, scores, -jnp.inf)
    own_place = lax.broadcasted_iota(i32, (rows, HALF), 1)
    own_scores = jnp.where(own_place == stream, own_scores, -jnp.inf)
    row_max = jnp.maximum(
        jnp.max(scores, axis=-1, keepdims=True), jnp.max(own_scores, axis=-1, keepdims=True)
    )
    weights = jnp.exp(scores - row_max)
    own_weights = jnp.exp(own_scores - row_max)
    total = jnp.sum(weights, axis=-1, keepdims=True) + jnp.sum(own_weights, axis=-1, keepdims=True)
    share = 1.0 / total
    mixed = jnp.dot((weights * share).astype(bf16), pairs, preferred_element_type=f32)
    mixed = mixed + jnp.dot(
        (own_weights * share).astype(bf16), pair_new, preferred_element_type=f32
    )
    mixed = mixed[:, HD:].astype(bf16)
    heads = jnp.concatenate([mixed[r * HALF : (r + 1) * HALF] for r in range(RATIO)], axis=1)
    for j in range(shards):
        span = slice(j * block, (j + 1) * block)
        own = jnp.dot(heads, o_own[:, span], preferred_element_type=f32)
        oth = jnp.dot(heads, o_oth[:, span], preferred_element_type=f32)
        out_ref[j, :, :block] = own.astype(bf16)
        out_ref[j, :, block:] = oth.astype(bf16)


def pack_kernel(rows_src, gain_src, adapt_src, books_src, out_ref, gain_ref, semaphores):
    columns, entries = adapt_src.shape[1:]
    tables = [adapt_src.at[i] for i in range(adapt_src.shape[0])]
    tables += [books_src.at[q] for q in range(NQ)]
    below = pl.ds(B, columns)
    copies = [pltpu.make_async_copy(gain_src, gain_ref, semaphores.at[0])]
    copies += [pltpu.make_async_copy(rows_src, out_ref.at[:B], semaphores.at[1])]
    for i, source in enumerate(tables):
        target = out_ref.at[below, pl.ds(i * entries, entries)]
        copies += [pltpu.make_async_copy(source, target, semaphores.at[2 + i])]
    for copy in copies:
        copy.start()
    start = len(tables) * entries
    free = out_ref.shape[1] - start
    copies[0].wait()
    gain = gain_ref[...].astype(f32)
    pieces = [gain[:, j : j + free] for j in range(0, gain.shape[1], free)]
    pieces += [jnp.zeros((columns - len(pieces), free), f32)]
    out_ref[B:, start:] = jnp.concatenate(pieces, axis=0).astype(bf16)
    for copy in copies[1:]:
        copy.wait()


def unpacked_gain(packed_ref):
    width = packed_ref.shape[1]
    start = (2 + NQ) * (width // 8)
    held = packed_ref[B:, start:].astype(f32)
    count = width // (width - start)
    return jnp.concatenate([held[j : j + 1] for j in range(count)], axis=1)


def load_kernel(*refs):
    count = (len(refs) - 1) // 2
    copies = [
        pltpu.make_async_copy(refs[i], refs[count + i], refs[-1].at[i]) for i in range(count)
    ]
    for copy in copies:
        copy.start()
    for copy in copies:
        copy.wait()


def first_kernel(
    place_ref, lengths_ref, packed_own, packed_oth, w_own, w_oth, o_own, o_oth, cache_ref,
    out_ref, shard_ref, g_own_ref, g_oth_ref,
):
    side, column = place_ref[0], place_ref[2]
    block = shard_ref.shape[1] // 2
    mine = pl.ds(pl.multiple_of(side * HALF, HALF), HALF)
    own = packed_own[mine, :].astype(f32)
    oth = packed_oth[mine, :].astype(f32)
    squares = jnp.sum(own * own + oth * oth, axis=-1, keepdims=True)
    gains = [unpacked_gain(packed_own), unpacked_gain(packed_oth)]
    g_own_ref[...], g_oth_ref[...] = gains
    part = pl.ds(pl.multiple_of(column * block, block), block)
    shard_ref[:, :block] = packed_own[mine, part]
    shard_ref[:, block:] = packed_oth[mine, part]
    scaled = (own * gains[0]).astype(bf16)
    proj = jnp.dot(scaled, w_own[...], preferred_element_type=f32)
    scaled = (oth * gains[1]).astype(bf16)
    proj = proj + jnp.dot(scaled, w_oth[...], preferred_element_type=f32)
    proj = proj * lax.rsqrt(squares / D + epsilon)
    ends = last_visible(0, place_ref, lengths_ref)
    attention_terms(proj, ends, o_own, o_oth, cache_ref.at[0], out_ref)


def later_kernel(
    tick, place_ref, lengths_ref, g_own, g_oth, w_own, w_oth, o_own, o_oth, cache_ref, x_ref,
    out_ref, inverse_ref,
):
    shards, block = x_ref.shape[0], x_ref.shape[2] // 2
    squares = jnp.zeros(x_ref.shape[1:], f32)
    proj = jnp.zeros((HALF, w_own.shape[1]), f32)
    for j in range(shards):
        span = slice(j * block, (j + 1) * block)
        rows = x_ref[j].astype(f32)
        squares = squares + rows * rows
        own = (rows[:, :block] * g_own[:, span]).astype(bf16)
        oth = (rows[:, block:] * g_oth[:, span]).astype(bf16)
        proj = proj + jnp.dot(own, w_own[span, :], preferred_element_type=f32)
        proj = proj + jnp.dot(oth, w_oth[span, :], preferred_element_type=f32)
    inverse_rms = lax.rsqrt(jnp.sum(squares, axis=-1, keepdims=True) / D + epsilon)
    inverse_ref[...] = jnp.broadcast_to(inverse_rms, inverse_ref.shape)
    proj = proj * inverse_rms
    ends = last_visible(tick, place_ref, lengths_ref)
    attention_terms(proj, ends, o_own, o_oth, cache_ref.at[tick], out_ref)


def sum_kernel(tick, place_ref, got_ref, shard_ref, inverse_ref, out_ref):
    section = place_ref[1]
    shard = shard_ref[...].astype(f32)
    total = shard
    for j in range(got_ref.shape[0]):
        total = total + got_ref[j].astype(f32)
    if tick:
        passed = shard * jnp.where(section == tick - 1, inverse_ref[:, :1], 1.0)
        total = jnp.where(section >= tick, total, passed)
    out_ref[...] = total.astype(bf16)


def last_sum_kernel(
    place_ref, got_ref, shard_ref, inverse_ref, early_0, early_1, early_2, out_ref, latest_ref
):
    sum_kernel(EARLY, place_ref, got_ref, shard_ref, inverse_ref, out_ref)
    section = place_ref[1]
    latest = out_ref[...].astype(f32)
    for tick, early in ((2, early_2), (1, early_1), (0, early_0)):
        latest = jnp.where(section <= tick, early[...].astype(f32), latest)
    latest_ref[...] = latest.astype(bf16)


def talk_kernel(
    place_ref, rows_ref, latest_ref, talk_gain, packed_own, packed_oth, codes_ref, out_ref
):
    side, column = place_ref[0], place_ref[2]
    block = rows_ref.shape[2] // 2
    columns, entries = packed_own.shape[0] - B, packed_own.shape[1] // 8
    first = side == 0
    gains = talk_gain[...].astype(f32)

    def halves(rows):
        own, oth = rows[:, :block].astype(f32), rows[:, block:].astype(f32)
        return jnp.where(first, own, oth), jnp.where(first, oth, own)

    def table(i):
        span = slice(i * entries, (i + 1) * entries)
        own, oth = packed_own[B:, span].astype(f32), packed_oth[B:, span].astype(f32)
        both = [jnp.where(first, own, oth), jnp.where(first, oth, own)]
        return jnp.concatenate(both, axis=0).astype(bf16)

    def beside(terms, tick):
        terms = terms[:, tick * HALF : (tick + 1) * HALF]
        return jnp.concatenate([terms[:columns], terms[columns:]], axis=1)

    def my_ids(tick, q):
        ids = codes_ref[tick, q : q + 1, :]
        return jnp.where(first, ids[:, :HALF], ids[:, HALF:]) - column * entries

    embedded = jnp.zeros((2 * columns, TICKS * HALF), f32)
    for q in range(NQ):
        ids = jnp.concatenate([my_ids(tick, q) for tick in range(TICKS)], axis=1)
        hot = lax.broadcasted_iota(i32, (entries, TICKS * HALF), 0) == ids
        hot = jnp.where(hot, 1.0, 0.0).astype(bf16)
        embedded = embedded + jnp.dot(table(2 + q), hot, preferred_element_type=f32)
    adapted = jnp.zeros((2 * columns, TICKS * HALF), f32)
    low, high = halves(rows_ref[...].reshape(TICKS * HALF, 2 * block))
    for i, part in enumerate((low, high)):
        scaled = (part * gains[i : i + 1]).astype(bf16)
        adapted = adapted + lax.dot_general(
            table(i), scaled, CONTRACT_LAST, preferred_element_type=f32
        )
    low, high = low[EARLY * HALF :], high[EARLY * HALF :]
    both = adapted + embedded
    pieces = [beside(both, tick) for tick in range(EARLY)]
    pieces += [beside(adapted, EARLY), beside(embedded, EARLY)]
    squares = jnp.sum(low * low + high * high, axis=1, keepdims=True)
    squares = jnp.concatenate([squares, squares], axis=0)
    upper = squares.astype(bf16).astype(f32)
    grid = jnp.concatenate(pieces, axis=0)
    grid = jnp.concatenate([grid, jnp.zeros((grid.shape[0], LANES - B), f32)], axis=1)
    grid = jnp.concatenate([grid, jnp.zeros((2 * LANES - grid.shape[0], LANES), f32)], axis=0)
    grid = grid.T[:B]
    lane = lax.broadcasted_iota(i32, grid.shape, 1)
    grid = jnp.where(lane == (TICKS + 1) * columns, upper, grid)
    grid = jnp.where(lane == (TICKS + 1) * columns + 1, squares - upper, grid)
    for c, part in enumerate(halves(latest_ref[...])):
        out_ref[c, :HALF] = grid[c * HALF : (c + 1) * HALF].astype(bf16)
        out_ref[c, HALF:] = part.astype(bf16)


def finish_kernel(got_ref, out_ref, leaving_ref):
    columns, block = out_ref.shape[1], got_ref.shape[2]
    shards = got_ref.shape[0] // 2
    tables = []
    for c in range(2):
        table = got_ref[c * shards, :HALF].astype(f32)
        for j in range(1, shards):
            table = table + got_ref[c * shards + j, :HALF].astype(f32)
        tables.append(table)
        for j in range(shards):
            rows = got_ref[c * shards + j, HALF:].astype(f32)
            leaving_ref[c * HALF : (c + 1) * HALF, j * block : (j + 1) * block] = rows
    table = jnp.concatenate(tables, axis=0)
    table = jnp.concatenate([table, jnp.zeros((LANES - B, block), f32)], axis=0).T
    for tick in range(EARLY):
        out_ref[tick] = table[tick * columns : (tick + 1) * columns, :B]
    base, at = EARLY * columns, (TICKS + 1) * columns
    squares = table[at : at + 1, :] + table[at + 1 : at + 2, :]
    rows = table[base : base + columns] * lax.rsqrt(squares / D + epsilon)
    rows = rows + table[base + columns : base + 2 * columns]
    out_ref[EARLY] = rows[:, :B]


def run(kernel, outs, *operands, scalars=True, limit=16):
    specs = [pl.BlockSpec(memory_space=pltpu.VMEM)] * len(operands)
    if scalars:
        specs[0] = pl.BlockSpec(memory_space=pltpu.SMEM)
    out_specs = jax.tree.map(lambda _: pl.BlockSpec(memory_space=pltpu.VMEM), outs)
    return pl.pallas_call(
        kernel,
        out_shape=outs,
        in_specs=specs,
        out_specs=out_specs,
        compiler_params=pltpu.CompilerParams(vmem_limit_bytes=limit * 2**20),
    )(*operands)


def shaped(*shape, dtype=bf16):
    return jax.ShapeDtypeStruct(shape, dtype)


SECTION = ("line", "place", "core")
LINES, PLACES = 8, 4
LINE = 2 * PLACES


def to_partner(value):
    return lax.ppermute(value, "core", [(0, 1), (1, 0)])


def to_next(value, tick):
    count, kept = LINES * LINE, 2 * tick
    pairs = [(i, i) for i in range(kept)] + [(i, i + 2) for i in range(kept, count - 2)]
    return lax.ppermute(value, SECTION, pairs + [(count - 2 + c, kept + c) for c in range(2)])


def exchange(blocks, axis="tp"):
    return lax.all_to_all(blocks, axis, 0, 0, tiled=True)


def replicate(block, count):
    return jnp.broadcast_to(block[None], (count,) + block.shape)


def across_lines(value, line):
    home = [LINES - 1 if place == EARLY else 0 for place in range(PLACES)]

    def sent(rows, *hops):
        at = lambda i, d: (home[i // 2] + d) % LINES * LINE + i
        pairs = [(at(i, start), at(i, end)) for start, end in hops for i in range(LINE)]
        return lax.ppermute(rows, SECTION, pairs)

    place = lax.axis_index("place")
    offset = lax.rem(line - jnp.where(place == EARLY, LINES - 1, 0) + LINES, LINES)
    some = jnp.where(offset == 0, value, jnp.zeros_like(value))
    some = some + sent(value, (0, 7)) + sent(value, (0, 1))
    return some + sent(some, (1, 2), (7, 6)) + sent(some, (0, 4), (1, 3), (7, 5))


def body(arriving, norm_gain, w_qkv, w_out, cache, lengths, talk_gain, w_adapt, codebooks, codes):
    position = lax.axis_index(SECTION)
    column = lax.axis_index("tp")
    shards = lax.axis_size("tp")
    section = position // 2
    width = arriving.shape[2]
    block = width // shards
    columns = w_adapt.shape[2]
    place = jnp.stack([lax.rem(position, 2), section, column]).astype(i32)

    w_own, o_own = w_qkv[0], w_out[0]
    w_oth = to_partner(w_own)
    o_oth = to_partner(o_own)
    there = pl.BlockSpec(memory_space=pltpu.HBM)
    here = pl.BlockSpec(memory_space=pltpu.VMEM)
    sources = [arriving[0], norm_gain, w_adapt.transpose(0, 2, 1), codebooks.transpose(0, 2, 1)]
    packed_own = pl.pallas_call(
        pack_kernel,
        out_shape=shaped(B + columns, width),
        in_specs=[there] * len(sources),
        out_specs=here,
        scratch_shapes=[
            pltpu.VMEM(norm_gain.shape, bf16), pltpu.SemaphoreType.DMA((4 + NQ,))
        ],
        compiler_params=pltpu.CompilerParams(vmem_limit_bytes=8 * 2**20),
    )(*(pltpu.with_memory_space_constraint(v, pltpu.HBM) for v in sources))
    packed_oth = to_partner(packed_own)
    cache_rows = cache[0].reshape(TICKS, HALF * CACHE, -1)
    blocks = shaped(shards, HALF, 2 * block)
    piece = shaped(HALF, 2 * block)

    sources, _ = lax.optimization_barrier(([lengths, w_own, o_own, cache_rows], packed_own))
    lengths, w_own, o_own, cache_rows = pl.pallas_call(
        load_kernel,
        out_shape=tuple(shaped(*v.shape, dtype=v.dtype) for v in sources),
        in_specs=[there] * len(sources),
        out_specs=(here,) * len(sources),
        scratch_shapes=[pltpu.SemaphoreType.DMA((len(sources),))],
        compiler_params=pltpu.CompilerParams(vmem_limit_bytes=8 * 2**20),
        cost_estimate=pl.CostEstimate(flops=0, bytes_accessed=7 * 2**20, transcendentals=0),
    )(*(pltpu.with_memory_space_constraint(v, pltpu.HBM) for v in sources))
    weights = (w_own, w_oth, o_own, o_oth, cache_rows)
    gain = shaped(1, width, dtype=f32)
    terms, shard, g_own, g_oth = run(
        first_kernel, (blocks, piece, gain, gain), place, lengths, packed_own, packed_oth, *weights
    )
    shared = (place, lengths, g_own, g_oth, *weights)
    finals = []
    inverse = jnp.zeros((HALF, LANES), f32)
    for tick in range(EARLY):
        got = exchange(terms)
        finals.append(run(functools.partial(sum_kernel, tick), piece, place, got, shard, inverse))
        shard = to_next(finals[-1], tick)
        rows = exchange(replicate(shard, shards))
        terms, inverse = run(
            functools.partial(later_kernel, tick + 1),
            (blocks, shaped(HALF, LANES, dtype=f32)),
            *shared, rows,
        )
    got = exchange(terms)
    held_rows, latest = run(
        last_sum_kernel, (piece, piece), place, got, shard, inverse, *finals
    )

    talk_rows = across_lines(held_rows, lax.axis_index("line"))
    talk_rows = exchange(replicate(talk_rows, PLACES), "place")
    payload = run(
        talk_kernel,
        shaped(2, B, block),
        place, talk_rows, latest, talk_gain, packed_own, packed_oth, codes.transpose(0, 2, 1),
    )
    payload = jnp.broadcast_to(payload[:, None], (2, shards, B, block))
    sums = exchange(payload.reshape(2 * shards, B, block), ("core", "tp"))
    talk, leaving = run(
        finish_kernel,
        (shaped(TICKS, columns, B, dtype=f32), shaped(B, width, dtype=f32)),
        sums,
        scalars=False,
    )
    return (leaving[None], talk.transpose(0, 2, 1))


def solution(mesh):
    devices = mesh.devices
    grid = jax.sharding.Mesh(
        devices.reshape(LINES, PLACES, 2, devices.shape[1]), SECTION + ("tp",)
    )
    placed = (
        P(SECTION, None, None),
        P(SECTION, None),
        P(SECTION, None, "tp"),
        P(SECTION, "tp", None),
        P(SECTION, None, None, None, "tp"),
        P(),
        P(None, "tp"),
        P(None, "tp", SECTION),
        P(None, "tp", SECTION),
        P(),
    )
    return jax.shard_map(
        body,
        mesh=grid,
        in_specs=placed,
        out_specs=(P(SECTION, None, None), P(None, None, SECTION)),
        check_vma=False,
    )
```

```python
import functools

import jax
import jax.numpy as jnp
from jax import lax
from jax.experimental import pallas as pl
from jax.experimental.pallas import tpu as pltpu
from jax.sharding import PartitionSpec as P

D = 4096
H = 32
KVH = 8
HD = 64
NQ = 4
TICKS = 4
B = 96
CACHE = 16
HALF = B // 2
RATIO = H // KVH
EARLY = TICKS - 1
LANES = 128

epsilon = 1e-05
f32 = jnp.float32
bf16 = jnp.bfloat16
i32 = jnp.int32
CONTRACT_LAST = (((1,), (1,)), ((), ()))


def last_visible(tick, place_ref, lengths_ref):
    side, section = place_ref[0], place_ref[1]
    lens = lengths_ref[pl.ds(jnp.maximum(section - tick, 0), 1), :]
    row = lax.broadcasted_iota(i32, (HALF, B), 0)
    lane = lax.broadcasted_iota(i32, (HALF, B), 1)
    lens = jnp.where(lane == row + side * HALF, lens, 0)
    lens = jnp.sum(lens, axis=1, keepdims=True)
    ends = lens + lax.broadcasted_iota(i32, (HALF, 1), 0) * CACHE
    return jnp.concatenate([ends] * RATIO, axis=0)


def attention_terms(proj, ends, o_own, o_oth, pairs_ref, out_ref):
    shards, block = out_ref.shape[0], out_ref.shape[2] // 2
    stacked = jnp.concatenate([proj[:, r * HD : (r + 1) * HD] for r in range(RATIO)], axis=0)
    queries = (stacked.astype(bf16).astype(f32) * (HD**-0.5)).astype(bf16)
    queries = jnp.concatenate([queries, jnp.zeros_like(queries)], axis=1)
    pair_new = proj[:, RATIO * HD :].astype(bf16)
    pairs = pairs_ref[...]
    scores = lax.dot_general(queries, pairs, CONTRACT_LAST, preferred_element_type=f32)
    own_scores = lax.dot_general(queries, pair_new, CONTRACT_LAST, preferred_element_type=f32)
    rows = RATIO * HALF
    stream = lax.rem(lax.broadcasted_iota(i32, (rows, 1), 0), HALF)
    place = lax.broadcasted_iota(i32, (rows, HALF * CACHE), 1)
    visible = jnp.logical_and(place >= stream * CACHE, place < ends)
    scores = jnp.where(visible, scores, -jnp.inf)
    own_place = lax.broadcasted_iota(i32, (rows, HALF), 1)
    own_scores = jnp.where(own_place == stream, own_scores, -jnp.inf)
    row_max = jnp.maximum(
        jnp.max(scores, axis=-1, keepdims=True), jnp.max(own_scores, axis=-1, keepdims=True)
    )
    weights = jnp.exp(scores - row_max)
    own_weights = jnp.exp(own_scores - row_max)
    total = jnp.sum(weights, axis=-1, keepdims=True) + jnp.sum(own_weights, axis=-1, keepdims=True)
    share = 1.0 / total
    mixed = jnp.dot((weights * share).astype(bf16), pairs, preferred_element_type=f32)
    mixed = mixed + jnp.dot(
        (own_weights * share).astype(bf16), pair_new, preferred_element_type=f32
    )
    mixed = mixed[:, HD:].astype(bf16)
    heads = jnp.concatenate([mixed[r * HALF : (r + 1) * HALF] for r in range(RATIO)], axis=1)
    for j in range(shards):
        span = slice(j * block, (j + 1) * block)
        own = jnp.dot(heads, o_own[:, span], preferred_element_type=f32)
        oth = jnp.dot(heads, o_oth[:, span], preferred_element_type=f32)
        out_ref[j, :, :block] = own.astype(bf16)
        out_ref[j, :, block:] = oth.astype(bf16)


def pack_kernel(gain_ref, rows_src, adapt_src, books_src, out_ref, semaphores):
    columns, entries = adapt_src.shape[1:]
    tables = [adapt_src.at[i] for i in range(adapt_src.shape[0])]
    tables += [books_src.at[q] for q in range(NQ)]
    below = pl.ds(B, columns)
    copies = [pltpu.make_async_copy(rows_src, out_ref.at[:B], semaphores.at[0])]
    for i, source in enumerate(tables):
        target = out_ref.at[below, pl.ds(i * entries, entries)]
        copies += [pltpu.make_async_copy(source, target, semaphores.at[1 + i])]
    for copy in copies:
        copy.start()
    start = len(tables) * entries
    free = out_ref.shape[1] - start
    gain = gain_ref[...].astype(f32)
    pieces = [gain[:, j : j + free] for j in range(0, gain.shape[1], free)]
    pieces += [jnp.zeros((columns - len(pieces), free), f32)]
    out_ref[B:, start:] = jnp.concatenate(pieces, axis=0).astype(bf16)
    for copy in copies:
        copy.wait()


def unpacked_gain(packed_ref):
    width = packed_ref.shape[1]
    start = (2 + NQ) * (width // 8)
    held = packed_ref[B:, start:].astype(f32)
    count = width // (width - start)
    return jnp.concatenate([held[j : j + 1] for j in range(count)], axis=1)


def load_kernel(*refs):
    count = (len(refs) - 1) // 2
    copies = [
        pltpu.make_async_copy(refs[i], refs[count + i], refs[-1].at[i]) for i in range(count)
    ]
    for copy in copies:
        copy.start()
    for copy in copies:
        copy.wait()


def first_kernel(
    place_ref, lengths_ref, packed_own, packed_oth, w_own, w_oth, o_own, o_oth, cache_ref,
    out_ref, shard_ref, g_own_ref, g_oth_ref,
):
    side, column = place_ref[0], place_ref[2]
    block = shard_ref.shape[1] // 2
    mine = pl.ds(pl.multiple_of(side * HALF, HALF), HALF)
    own = packed_own[mine, :].astype(f32)
    oth = packed_oth[mine, :].astype(f32)
    squares = jnp.sum(own * own + oth * oth, axis=-1, keepdims=True)
    gains = [unpacked_gain(packed_own), unpacked_gain(packed_oth)]
    g_own_ref[...], g_oth_ref[...] = gains
    part = pl.ds(pl.multiple_of(column * block, block), block)
    shard_ref[:, :block] = packed_own[mine, part]
    shard_ref[:, block:] = packed_oth[mine, part]
    scaled = (own * gains[0]).astype(bf16)
    proj = jnp.dot(scaled, w_own[...], preferred_element_type=f32)
    scaled = (oth * gains[1]).astype(bf16)
    proj = proj + jnp.dot(scaled, w_oth[...], preferred_element_type=f32)
    proj = proj * lax.rsqrt(squares / D + epsilon)
    ends = last_visible(0, place_ref, lengths_ref)
    attention_terms(proj, ends, o_own, o_oth, cache_ref.at[0], out_ref)


def later_kernel(
    tick, place_ref, lengths_ref, g_own, g_oth, w_own, w_oth, o_own, o_oth, cache_ref, x_ref,
    out_ref, inverse_ref,
):
    shards, block = x_ref.shape[0], x_ref.shape[2] // 2
    squares = jnp.zeros(x_ref.shape[1:], f32)
    proj = jnp.zeros((HALF, w_own.shape[1]), f32)
    for j in range(shards):
        span = slice(j * block, (j + 1) * block)
        rows = x_ref[j].astype(f32)
        squares = squares + rows * rows
        own = (rows[:, :block] * g_own[:, span]).astype(bf16)
        oth = (rows[:, block:] * g_oth[:, span]).astype(bf16)
        proj = proj + jnp.dot(own, w_own[span, :], preferred_element_type=f32)
        proj = proj + jnp.dot(oth, w_oth[span, :], preferred_element_type=f32)
    inverse_rms = lax.rsqrt(jnp.sum(squares, axis=-1, keepdims=True) / D + epsilon)
    inverse_ref[...] = jnp.broadcast_to(inverse_rms, inverse_ref.shape)
    proj = proj * inverse_rms
    ends = last_visible(tick, place_ref, lengths_ref)
    attention_terms(proj, ends, o_own, o_oth, cache_ref.at[tick], out_ref)


def sum_kernel(tick, place_ref, got_ref, shard_ref, inverse_ref, out_ref):
    section = place_ref[1]
    shard = shard_ref[...].astype(f32)
    total = shard
    for j in range(got_ref.shape[0]):
        total = total + got_ref[j].astype(f32)
    if tick:
        passed = shard * jnp.where(section == tick - 1, inverse_ref[:, :1], 1.0)
        total = jnp.where(section >= tick, total, passed)
    out_ref[...] = total.astype(bf16)


def last_sum_kernel(
    place_ref, got_ref, shard_ref, inverse_ref, early_0, early_1, early_2, out_ref, latest_ref
):
    sum_kernel(EARLY, place_ref, got_ref, shard_ref, inverse_ref, out_ref)
    section = place_ref[1]
    latest = out_ref[...].astype(f32)
    for tick, early in ((2, early_2), (1, early_1), (0, early_0)):
        latest = jnp.where(section <= tick, early[...].astype(f32), latest)
    latest_ref[...] = latest.astype(bf16)


def talk_kernel(
    place_ref, rows_ref, latest_ref, talk_gain, packed_own, packed_oth, codes_ref, out_ref
):
    side, column = place_ref[0], place_ref[2]
    block = rows_ref.shape[2] // 2
    columns, entries = packed_own.shape[0] - B, packed_own.shape[1] // 8
    first = side == 0
    gains = talk_gain[...].astype(f32)

    def halves(rows):
        own, oth = rows[:, :block].astype(f32), rows[:, block:].astype(f32)
        return jnp.where(first, own, oth), jnp.where(first, oth, own)

    def table(i):
        span = slice(i * entries, (i + 1) * entries)
        own, oth = packed_own[B:, span].astype(f32), packed_oth[B:, span].astype(f32)
        both = [jnp.where(first, own, oth), jnp.where(first, oth, own)]
        return jnp.concatenate(both, axis=0).astype(bf16)

    def beside(terms, tick):
        terms = terms[:, tick * HALF : (tick + 1) * HALF]
        return jnp.concatenate([terms[:columns], terms[columns:]], axis=1)

    def my_ids(tick, q):
        ids = codes_ref[tick, q : q + 1, :]
        return jnp.where(first, ids[:, :HALF], ids[:, HALF:]) - column * entries

    embedded = jnp.zeros((2 * columns, TICKS * HALF), f32)
    for q in range(NQ):
        ids = jnp.concatenate([my_ids(tick, q) for tick in range(TICKS)], axis=1)
        hot = lax.broadcasted_iota(i32, (entries, TICKS * HALF), 0) == ids
        hot = jnp.where(hot, 1.0, 0.0).astype(bf16)
        embedded = embedded + jnp.dot(table(2 + q), hot, preferred_element_type=f32)
    adapted = jnp.zeros((2 * columns, TICKS * HALF), f32)
    low, high = halves(rows_ref[...].reshape(TICKS * HALF, 2 * block))
    for i, part in enumerate((low, high)):
        scaled = (part * gains[i : i + 1]).astype(bf16)
        adapted = adapted + lax.dot_general(
            table(i), scaled, CONTRACT_LAST, preferred_element_type=f32
        )
    low, high = low[EARLY * HALF :], high[EARLY * HALF :]
    both = adapted + embedded
    pieces = [beside(both, tick) for tick in range(EARLY)]
    pieces += [beside(adapted, EARLY), beside(embedded, EARLY)]
    squares = jnp.sum(low * low + high * high, axis=1, keepdims=True)
    squares = jnp.concatenate([squares, squares], axis=0)
    upper = squares.astype(bf16).astype(f32)
    grid = jnp.concatenate(pieces, axis=0)
    grid = jnp.concatenate([grid, jnp.zeros((grid.shape[0], LANES - B), f32)], axis=1)
    grid = jnp.concatenate([grid, jnp.zeros((2 * LANES - grid.shape[0], LANES), f32)], axis=0)
    grid = grid.T[:B]
    lane = lax.broadcasted_iota(i32, grid.shape, 1)
    grid = jnp.where(lane == (TICKS + 1) * columns, upper, grid)
    grid = jnp.where(lane == (TICKS + 1) * columns + 1, squares - upper, grid)
    for c, part in enumerate(halves(latest_ref[...])):
        out_ref[c, :HALF] = grid[c * HALF : (c + 1) * HALF].astype(bf16)
        out_ref[c, HALF:] = part.astype(bf16)


def finish_kernel(got_ref, out_ref, leaving_ref):
    columns, block = out_ref.shape[1], got_ref.shape[2]
    shards = got_ref.shape[0] // 2
    tables = []
    for c in range(2):
        table = got_ref[c * shards, :HALF].astype(f32)
        for j in range(1, shards):
            table = table + got_ref[c * shards + j, :HALF].astype(f32)
        tables.append(table)
        for j in range(shards):
            rows = got_ref[c * shards + j, HALF:].astype(f32)
            leaving_ref[c * HALF : (c + 1) * HALF, j * block : (j + 1) * block] = rows
    table = jnp.concatenate(tables, axis=0)
    table = jnp.concatenate([table, jnp.zeros((LANES - B, block), f32)], axis=0).T
    for tick in range(EARLY):
        out_ref[tick] = table[tick * columns : (tick + 1) * columns, :B]
    base, at = EARLY * columns, (TICKS + 1) * columns
    squares = table[at : at + 1, :] + table[at + 1 : at + 2, :]
    rows = table[base : base + columns] * lax.rsqrt(squares / D + epsilon)
    rows = rows + table[base + columns : base + 2 * columns]
    out_ref[EARLY] = rows[:, :B]


def run(kernel, outs, *operands, scalars=True, limit=16):
    specs = [pl.BlockSpec(memory_space=pltpu.VMEM)] * len(operands)
    if scalars:
        specs[0] = pl.BlockSpec(memory_space=pltpu.SMEM)
    out_specs = jax.tree.map(lambda _: pl.BlockSpec(memory_space=pltpu.VMEM), outs)
    return pl.pallas_call(
        kernel,
        out_shape=outs,
        in_specs=specs,
        out_specs=out_specs,
        compiler_params=pltpu.CompilerParams(vmem_limit_bytes=limit * 2**20),
    )(*operands)


def shaped(*shape, dtype=bf16):
    return jax.ShapeDtypeStruct(shape, dtype)


SECTION = ("line", "place", "core")
LINES, PLACES = 8, 4
LINE = 2 * PLACES


def to_partner(value):
    return lax.ppermute(value, "core", [(0, 1), (1, 0)])


def to_next(value, tick):
    count, kept = LINES * LINE, 2 * tick
    pairs = [(i, i) for i in range(kept)] + [(i, i + 2) for i in range(kept, count - 2)]
    return lax.ppermute(value, SECTION, pairs + [(count - 2 + c, kept + c) for c in range(2)])


def exchange(blocks, axis="tp"):
    return lax.all_to_all(blocks, axis, 0, 0, tiled=True)


def replicate(block, count):
    return jnp.broadcast_to(block[None], (count,) + block.shape)


def across_lines(value, line):
    home = [LINES - 1 if place == EARLY else 0 for place in range(PLACES)]

    def sent(rows, *hops):
        at = lambda i, d: (home[i // 2] + d) % LINES * LINE + i
        pairs = [(at(i, start), at(i, end)) for start, end in hops for i in range(LINE)]
        return lax.ppermute(rows, SECTION, pairs)

    place = lax.axis_index("place")
    offset = lax.rem(line - jnp.where(place == EARLY, LINES - 1, 0) + LINES, LINES)
    some = jnp.where(offset == 0, value, jnp.zeros_like(value))
    some = some + sent(value, (0, 7)) + sent(value, (0, 1))
    return some + sent(some, (1, 2), (7, 6)) + sent(some, (0, 4), (1, 3), (7, 5))


def body(arriving, norm_gain, w_qkv, w_out, cache, lengths, talk_gain, w_adapt, codebooks, codes):
    position = lax.axis_index(SECTION)
    column = lax.axis_index("tp")
    shards = lax.axis_size("tp")
    section = position // 2
    width = arriving.shape[2]
    block = width // shards
    columns = w_adapt.shape[2]
    place = jnp.stack([lax.rem(position, 2), section, column]).astype(i32)

    w_own, o_own = w_qkv[0], w_out[0]
    w_oth = to_partner(w_own)
    o_oth = to_partner(o_own)
    there = pl.BlockSpec(memory_space=pltpu.HBM)
    here = pl.BlockSpec(memory_space=pltpu.VMEM)
    sources = [arriving[0], w_adapt.transpose(0, 2, 1), codebooks.transpose(0, 2, 1)]
    packed_own = pl.pallas_call(
        pack_kernel,
        out_shape=shaped(B + columns, width),
        in_specs=[here] + [there] * len(sources),
        out_specs=here,
        scratch_shapes=[pltpu.SemaphoreType.DMA((3 + NQ,))],
        compiler_params=pltpu.CompilerParams(vmem_limit_bytes=8 * 2**20),
    )(norm_gain, *(pltpu.with_memory_space_constraint(v, pltpu.HBM) for v in sources))
    packed_oth = to_partner(packed_own)
    cache_rows = cache[0].reshape(TICKS, HALF * CACHE, -1)
    blocks = shaped(shards, HALF, 2 * block)
    piece = shaped(HALF, 2 * block)

    sources, _ = lax.optimization_barrier(([lengths, w_own, o_own, cache_rows], packed_own))
    lengths, w_own, o_own, cache_rows = pl.pallas_call(
        load_kernel,
        out_shape=tuple(shaped(*v.shape, dtype=v.dtype) for v in sources),
        in_specs=[there] * len(sources),
        out_specs=(here,) * len(sources),
        scratch_shapes=[pltpu.SemaphoreType.DMA((len(sources),))],
        compiler_params=pltpu.CompilerParams(vmem_limit_bytes=8 * 2**20),
        cost_estimate=pl.CostEstimate(flops=0, bytes_accessed=7 * 2**20, transcendentals=0),
    )(*(pltpu.with_memory_space_constraint(v, pltpu.HBM) for v in sources))
    weights = (w_own, w_oth, o_own, o_oth, cache_rows)
    gain = shaped(1, width, dtype=f32)
    terms, shard, g_own, g_oth = run(
        first_kernel, (blocks, piece, gain, gain), place, lengths, packed_own, packed_oth, *weights
    )
    shared = (place, lengths, g_own, g_oth, *weights)
    finals = []
    inverse = jnp.zeros((HALF, LANES), f32)
    for tick in range(EARLY):
        got = exchange(terms)
        finals.append(run(functools.partial(sum_kernel, tick), piece, place, got, shard, inverse))
        shard = to_next(finals[-1], tick)
        rows = exchange(replicate(shard, shards))
        terms, inverse = run(
            functools.partial(later_kernel, tick + 1),
            (blocks, shaped(HALF, LANES, dtype=f32)),
            *shared, rows,
        )
    got = exchange(terms)
    held_rows, latest = run(
        last_sum_kernel, (piece, piece), place, got, shard, inverse, *finals
    )

    talk_rows = across_lines(held_rows, lax.axis_index("line"))
    talk_rows = exchange(replicate(talk_rows, PLACES), "place")
    payload = run(
        talk_kernel,
        shaped(2, B, block),
        place, talk_rows, latest, talk_gain, packed_own, packed_oth, codes.transpose(0, 2, 1),
    )
    payload = jnp.broadcast_to(payload[:, None], (2, shards, B, block))
    sums = exchange(payload.reshape(2 * shards, B, block), ("core", "tp"))
    talk, leaving = run(
        finish_kernel,
        (shaped(TICKS, columns, B, dtype=f32), shaped(B, width, dtype=f32)),
        sums,
        scalars=False,
    )
    return (leaving[None], talk.transpose(0, 2, 1))


def solution(mesh):
    devices = mesh.devices
    grid = jax.sharding.Mesh(
        devices.reshape(LINES, PLACES, 2, devices.shape[1]), SECTION + ("tp",)
    )
    placed = (
        P(SECTION, None, None),
        P(SECTION, None),
        P(SECTION, None, "tp"),
        P(SECTION, "tp", None),
        P(SECTION, None, None, None, "tp"),
        P(),
        P(None, "tp"),
        P(None, "tp", SECTION),
        P(None, "tp", SECTION),
        P(),
    )
    return jax.shard_map(
        body,
        mesh=grid,
        in_specs=placed,
        out_specs=(P(SECTION, None, None), P(None, None, SECTION)),
        check_vma=False,
    )
```

```python
import functools

import jax
import jax.numpy as jnp
from jax import lax
from jax.experimental import pallas as pl
from jax.experimental.pallas import tpu as pltpu
from jax.sharding import PartitionSpec as P

D = 4096
H = 32
KVH = 8
HD = 64
NQ = 4
TICKS = 4
B = 96
CACHE = 16
HALF = B // 2
RATIO = H // KVH
EARLY = TICKS - 1
LANES = 128

epsilon = 1e-05
f32 = jnp.float32
bf16 = jnp.bfloat16
i32 = jnp.int32
CONTRACT_LAST = (((1,), (1,)), ((), ()))


def last_visible(tick, place_ref, lengths_ref):
    side, section = place_ref[0], place_ref[1]
    lens = lengths_ref[pl.ds(jnp.maximum(section - tick, 0), 1), :]
    row = lax.broadcasted_iota(i32, (HALF, B), 0)
    lane = lax.broadcasted_iota(i32, (HALF, B), 1)
    lens = jnp.where(lane == row + side * HALF, lens, 0)
    lens = jnp.sum(lens, axis=1, keepdims=True)
    ends = lens + lax.broadcasted_iota(i32, (HALF, 1), 0) * CACHE
    return jnp.concatenate([ends] * RATIO, axis=0)


def attention_terms(proj, ends, o_own, o_oth, pairs_ref, out_ref):
    shards, block = out_ref.shape[0], out_ref.shape[2] // 2
    stacked = jnp.concatenate([proj[:, r * HD : (r + 1) * HD] for r in range(RATIO)], axis=0)
    queries = (stacked.astype(bf16).astype(f32) * (HD**-0.5)).astype(bf16)
    queries = jnp.concatenate([queries, jnp.zeros_like(queries)], axis=1)
    pair_new = proj[:, RATIO * HD :].astype(bf16)
    pairs = pairs_ref[...]
    scores = lax.dot_general(queries, pairs, CONTRACT_LAST, preferred_element_type=f32)
    beside_new = jnp.concatenate([pair_new.astype(f32)] * RATIO, axis=0)
    own_scores = jnp.sum(queries.astype(f32) * beside_new, axis=-1, keepdims=True)
    rows = RATIO * HALF
    stream = lax.rem(lax.broadcasted_iota(i32, (rows, 1), 0), HALF)
    place = lax.broadcasted_iota(i32, (rows, HALF * CACHE), 1)
    visible = jnp.logical_and(place >= stream * CACHE, place < ends)
    scores = jnp.where(visible, scores, -jnp.inf)
    row_max = jnp.maximum(jnp.max(scores, axis=-1, keepdims=True), own_scores)
    weights = jnp.exp(scores - row_max)
    own_weights = jnp.exp(own_scores - row_max)
    total = jnp.sum(weights, axis=-1, keepdims=True) + own_weights
    share = 1.0 / total
    mixed = jnp.dot((weights * share).astype(bf16), pairs, preferred_element_type=f32)
    mixed = mixed + (own_weights * share).astype(bf16).astype(f32) * beside_new
    mixed = mixed[:, HD:].astype(bf16)
    heads = jnp.concatenate([mixed[r * HALF : (r + 1) * HALF] for r in range(RATIO)], axis=1)
    for j in range(shards):
        span = slice(j * block, (j + 1) * block)
        own = jnp.dot(heads, o_own[:, span], preferred_element_type=f32)
        oth = jnp.dot(heads, o_oth[:, span], preferred_element_type=f32)
        out_ref[j, :, :block] = own.astype(bf16)
        out_ref[j, :, block:] = oth.astype(bf16)


def pack_kernel(gain_ref, rows_src, adapt_src, books_src, out_ref, semaphores):
    columns, entries = adapt_src.shape[1:]
    tables = [adapt_src.at[i] for i in range(adapt_src.shape[0])]
    tables += [books_src.at[q] for q in range(NQ)]
    below = pl.ds(B, columns)
    copies = [pltpu.make_async_copy(rows_src, out_ref.at[:B], semaphores.at[0])]
    for i, source in enumerate(tables):
        target = out_ref.at[below, pl.ds(i * entries, entries)]
        copies += [pltpu.make_async_copy(source, target, semaphores.at[1 + i])]
    for copy in copies:
        copy.start()
    start = len(tables) * entries
    free = out_ref.shape[1] - start
    gain = gain_ref[...].astype(f32)
    pieces = [gain[:, j : j + free] for j in range(0, gain.shape[1], free)]
    pieces += [jnp.zeros((columns - len(pieces), free), f32)]
    out_ref[B:, start:] = jnp.concatenate(pieces, axis=0).astype(bf16)
    for copy in copies:
        copy.wait()


def unpacked_gain(packed_ref):
    width = packed_ref.shape[1]
    start = (2 + NQ) * (width // 8)
    held = packed_ref[B:, start:].astype(f32)
    count = width // (width - start)
    return jnp.concatenate([held[j : j + 1] for j in range(count)], axis=1)


def load_kernel(*refs):
    count = (len(refs) - 1) // 2
    copies = [
        pltpu.make_async_copy(refs[i], refs[count + i], refs[-1].at[i]) for i in range(count)
    ]
    for copy in copies:
        copy.start()
    for copy in copies:
        copy.wait()


def first_kernel(
    place_ref, lengths_ref, packed_own, packed_oth, w_own, w_oth, o_own, o_oth, cache_ref,
    out_ref, shard_ref, g_own_ref, g_oth_ref,
):
    side, column = place_ref[0], place_ref[2]
    block = shard_ref.shape[1] // 2
    mine = pl.ds(pl.multiple_of(side * HALF, HALF), HALF)
    own = packed_own[mine, :].astype(f32)
    oth = packed_oth[mine, :].astype(f32)
    squares = jnp.sum(own * own + oth * oth, axis=-1, keepdims=True)
    gains = [unpacked_gain(packed_own), unpacked_gain(packed_oth)]
    g_own_ref[...], g_oth_ref[...] = gains
    part = pl.ds(pl.multiple_of(column * block, block), block)
    shard_ref[:, :block] = packed_own[mine, part]
    shard_ref[:, block:] = packed_oth[mine, part]
    scaled = (own * gains[0]).astype(bf16)
    proj = jnp.dot(scaled, w_own[...], preferred_element_type=f32)
    scaled = (oth * gains[1]).astype(bf16)
    proj = proj + jnp.dot(scaled, w_oth[...], preferred_element_type=f32)
    proj = proj * lax.rsqrt(squares / D + epsilon)
    ends = last_visible(0, place_ref, lengths_ref)
    attention_terms(proj, ends, o_own, o_oth, cache_ref.at[0], out_ref)


def later_kernel(
    tick, place_ref, lengths_ref, g_own, g_oth, w_own, w_oth, o_own, o_oth, cache_ref, x_ref,
    out_ref, inverse_ref,
):
    shards, block = x_ref.shape[0], x_ref.shape[2] // 2
    squares = jnp.zeros(x_ref.shape[1:], f32)
    proj = jnp.zeros((HALF, w_own.shape[1]), f32)
    for j in range(shards):
        span = slice(j * block, (j + 1) * block)
        rows = x_ref[j].astype(f32)
        squares = squares + rows * rows
        own = (rows[:, :block] * g_own[:, span]).astype(bf16)
        oth = (rows[:, block:] * g_oth[:, span]).astype(bf16)
        proj = proj + jnp.dot(own, w_own[span, :], preferred_element_type=f32)
        proj = proj + jnp.dot(oth, w_oth[span, :], preferred_element_type=f32)
    inverse_rms = lax.rsqrt(jnp.sum(squares, axis=-1, keepdims=True) / D + epsilon)
    inverse_ref[...] = jnp.broadcast_to(inverse_rms, inverse_ref.shape)
    proj = proj * inverse_rms
    ends = last_visible(tick, place_ref, lengths_ref)
    attention_terms(proj, ends, o_own, o_oth, cache_ref.at[tick], out_ref)


def sum_kernel(tick, place_ref, got_ref, shard_ref, inverse_ref, out_ref):
    section = place_ref[1]
    shard = shard_ref[...].astype(f32)
    total = shard
    for j in range(got_ref.shape[0]):
        total = total + got_ref[j].astype(f32)
    if tick:
        passed = shard * jnp.where(section == tick - 1, inverse_ref[:, :1], 1.0)
        total = jnp.where(section >= tick, total, passed)
    out_ref[...] = total.astype(bf16)


def last_sum_kernel(
    place_ref, got_ref, shard_ref, inverse_ref, early_0, early_1, early_2, out_ref, latest_ref
):
    sum_kernel(EARLY, place_ref, got_ref, shard_ref, inverse_ref, out_ref)
    section = place_ref[1]
    latest = out_ref[...].astype(f32)
    for tick, early in ((2, early_2), (1, early_1), (0, early_0)):
        latest = jnp.where(section <= tick, early[...].astype(f32), latest)
    latest_ref[...] = latest.astype(bf16)


def pair_table(i, first, packed_own, packed_oth):
    entries = packed_own.shape[1] // 8
    span = slice(i * entries, (i + 1) * entries)
    own, oth = packed_own[B:, span].astype(f32), packed_oth[B:, span].astype(f32)
    both = [jnp.where(first, own, oth), jnp.where(first, oth, own)]
    return jnp.concatenate(both, axis=0).astype(bf16)


def embed_kernel(place_ref, packed_own, packed_oth, codes_ref, out_ref):
    column, first = place_ref[2], place_ref[0] == 0
    entries = packed_own.shape[1] // 8
    embedded = jnp.zeros(out_ref.shape, f32)
    for q in range(NQ):
        ids = [codes_ref[tick, q : q + 1, :] for tick in range(TICKS)]
        ids = [jnp.where(first, row[:, :HALF], row[:, HALF:]) for row in ids]
        ids = jnp.concatenate(ids, axis=1) - column * entries
        hot = lax.broadcasted_iota(i32, (entries, TICKS * HALF), 0) == ids
        hot = jnp.where(hot, 1.0, 0.0).astype(bf16)
        table = pair_table(2 + q, first, packed_own, packed_oth)
        embedded = embedded + jnp.dot(table, hot, preferred_element_type=f32)
    out_ref[...] = embedded


def talk_kernel(
    place_ref, rows_ref, latest_ref, talk_gain, packed_own, packed_oth, embedded_ref, out_ref
):
    first = place_ref[0] == 0
    block = rows_ref.shape[2] // 2
    columns = packed_own.shape[0] - B
    gains = talk_gain[...].astype(f32)

    def halves(rows):
        own, oth = rows[:, :block].astype(f32), rows[:, block:].astype(f32)
        return jnp.where(first, own, oth), jnp.where(first, oth, own)

    def beside(terms, tick):
        terms = terms[:, tick * HALF : (tick + 1) * HALF]
        return jnp.concatenate([terms[:columns], terms[columns:]], axis=1)

    embedded = embedded_ref[...]
    adapted = jnp.zeros((2 * columns, TICKS * HALF), f32)
    low, high = halves(rows_ref[...].reshape(TICKS * HALF, 2 * block))
    for i, part in enumerate((low, high)):
        scaled = (part * gains[i : i + 1]).astype(bf16)
        adapted = adapted + lax.dot_general(
            pair_table(i, first, packed_own, packed_oth),
            scaled,
            CONTRACT_LAST,
            preferred_element_type=f32,
        )
    low, high = low[EARLY * HALF :], high[EARLY * HALF :]
    both = adapted + embedded
    pieces = [beside(both, tick) for tick in range(EARLY)]
    pieces += [beside(adapted, EARLY), beside(embedded, EARLY)]
    squares = jnp.sum(low * low + high * high, axis=1, keepdims=True)
    squares = jnp.concatenate([squares, squares], axis=0)
    upper = squares.astype(bf16).astype(f32)
    grid = jnp.concatenate(pieces, axis=0)
    grid = jnp.concatenate([grid, jnp.zeros((grid.shape[0], LANES - B), f32)], axis=1)
    grid = jnp.concatenate([grid, jnp.zeros((2 * LANES - grid.shape[0], LANES), f32)], axis=0)
    grid = grid.T[:B]
    lane = lax.broadcasted_iota(i32, grid.shape, 1)
    grid = jnp.where(lane == (TICKS + 1) * columns, upper, grid)
    grid = jnp.where(lane == (TICKS + 1) * columns + 1, squares - upper, grid)
    for c, part in enumerate(halves(latest_ref[...])):
        out_ref[c, :HALF] = grid[c * HALF : (c + 1) * HALF].astype(bf16)
        out_ref[c, HALF:] = part.astype(bf16)


def finish_kernel(got_ref, out_ref, leaving_ref):
    columns, block = out_ref.shape[1], got_ref.shape[2]
    shards = got_ref.shape[0] // 2
    tables = []
    for c in range(2):
        table = got_ref[c * shards, :HALF].astype(f32)
        for j in range(1, shards):
            table = table + got_ref[c * shards + j, :HALF].astype(f32)
        tables.append(table)
        for j in range(shards):
            rows = got_ref[c * shards + j, HALF:].astype(f32)
            leaving_ref[c * HALF : (c + 1) * HALF, j * block : (j + 1) * block] = rows
    table = jnp.concatenate(tables, axis=0)
    table = jnp.concatenate([table, jnp.zeros((LANES - B, block), f32)], axis=0).T
    for tick in range(EARLY):
        out_ref[tick] = table[tick * columns : (tick + 1) * columns, :B]
    base, at = EARLY * columns, (TICKS + 1) * columns
    squares = table[at : at + 1, :] + table[at + 1 : at + 2, :]
    rows = table[base : base + columns] * lax.rsqrt(squares / D + epsilon)
    rows = rows + table[base + columns : base + 2 * columns]
    out_ref[EARLY] = rows[:, :B]


def run(kernel, outs, *operands, scalars=True, limit=16):
    specs = [pl.BlockSpec(memory_space=pltpu.VMEM)] * len(operands)
    if scalars:
        specs[0] = pl.BlockSpec(memory_space=pltpu.SMEM)
    out_specs = jax.tree.map(lambda _: pl.BlockSpec(memory_space=pltpu.VMEM), outs)
    return pl.pallas_call(
        kernel,
        out_shape=outs,
        in_specs=specs,
        out_specs=out_specs,
        compiler_params=pltpu.CompilerParams(vmem_limit_bytes=limit * 2**20),
    )(*operands)


def shaped(*shape, dtype=bf16):
    return jax.ShapeDtypeStruct(shape, dtype)


SECTION = ("line", "place", "core")
LINES, PLACES = 8, 4
LINE = 2 * PLACES


def to_partner(value):
    return lax.ppermute(value, "core", [(0, 1), (1, 0)])


def to_next(value, tick):
    count, kept = LINES * LINE, 2 * tick
    pairs = [(i, i) for i in range(kept)] + [(i, i + 2) for i in range(kept, count - 2)]
    return lax.ppermute(value, SECTION, pairs + [(count - 2 + c, kept + c) for c in range(2)])


def exchange(blocks, axis="tp"):
    return lax.all_to_all(blocks, axis, 0, 0, tiled=True)


def replicate(block, count):
    return jnp.broadcast_to(block[None], (count,) + block.shape)


def across_lines(value, line):
    home = [LINES - 1 if place == EARLY else 0 for place in range(PLACES)]

    def sent(rows, *hops):
        at = lambda i, d: (home[i // 2] + d) % LINES * LINE + i
        pairs = [(at(i, start), at(i, end)) for start, end in hops for i in range(LINE)]
        return lax.ppermute(rows, SECTION, pairs)

    place = lax.axis_index("place")
    offset = lax.rem(line - jnp.where(place == EARLY, LINES - 1, 0) + LINES, LINES)
    some = jnp.where(offset == 0, value, jnp.zeros_like(value))
    far = sent(value, (0, 4))
    some = some + sent(value, (0, 7)) + sent(value, (0, 1))
    return some + sent(some, (1, 2), (7, 6)) + sent(some, (1, 3), (7, 5)) + far


def body(arriving, norm_gain, w_qkv, w_out, cache, lengths, talk_gain, w_adapt, codebooks, codes):
    position = lax.axis_index(SECTION)
    column = lax.axis_index("tp")
    shards = lax.axis_size("tp")
    section = position // 2
    width = arriving.shape[2]
    block = width // shards
    columns = w_adapt.shape[2]
    place = jnp.stack([lax.rem(position, 2), section, column]).astype(i32)

    w_own, o_own = w_qkv[0], w_out[0]
    w_oth = to_partner(w_own)
    o_oth = to_partner(o_own)
    there = pl.BlockSpec(memory_space=pltpu.HBM)
    here = pl.BlockSpec(memory_space=pltpu.VMEM)
    sources = [arriving[0], w_adapt.transpose(0, 2, 1), codebooks.transpose(0, 2, 1)]
    packed_own = pl.pallas_call(
        pack_kernel,
        out_shape=shaped(B + columns, width),
        in_specs=[here] + [there] * len(sources),
        out_specs=here,
        scratch_shapes=[pltpu.SemaphoreType.DMA((3 + NQ,))],
        compiler_params=pltpu.CompilerParams(vmem_limit_bytes=8 * 2**20),
    )(norm_gain, *(pltpu.with_memory_space_constraint(v, pltpu.HBM) for v in sources))
    packed_oth = to_partner(packed_own)
    cache_rows = cache[0].reshape(TICKS, HALF * CACHE, -1)
    blocks = shaped(shards, HALF, 2 * block)
    piece = shaped(HALF, 2 * block)

    sources, _ = lax.optimization_barrier(([lengths, w_own, o_own, cache_rows], packed_own))
    lengths, w_own, o_own, cache_rows = pl.pallas_call(
        load_kernel,
        out_shape=tuple(shaped(*v.shape, dtype=v.dtype) for v in sources),
        in_specs=[there] * len(sources),
        out_specs=(here,) * len(sources),
        scratch_shapes=[pltpu.SemaphoreType.DMA((len(sources),))],
        compiler_params=pltpu.CompilerParams(vmem_limit_bytes=8 * 2**20),
        cost_estimate=pl.CostEstimate(flops=0, bytes_accessed=7 * 2**20, transcendentals=0),
    )(*(pltpu.with_memory_space_constraint(v, pltpu.HBM) for v in sources))
    weights = (w_own, w_oth, o_own, o_oth, cache_rows)
    gain = shaped(1, width, dtype=f32)
    terms, shard, g_own, g_oth = run(
        first_kernel, (blocks, piece, gain, gain), place, lengths, packed_own, packed_oth, *weights
    )
    shared = (place, lengths, g_own, g_oth, *weights)
    finals = []
    inverse = jnp.zeros((HALF, LANES), f32)
    for tick in range(EARLY):
        got = exchange(terms)
        finals.append(run(functools.partial(sum_kernel, tick), piece, place, got, shard, inverse))
        shard = to_next(finals[-1], tick)
        if tick == 0:
            tokens, _ = lax.optimization_barrier((codes.transpose(0, 2, 1), finals[0]))
            embedded = run(
                embed_kernel, shaped(2 * columns, TICKS * HALF, dtype=f32),
                place, packed_own, packed_oth, tokens,
            )
            shard, embedded = lax.optimization_barrier((shard, embedded))
        rows = exchange(replicate(shard, shards))
        terms, inverse = run(
            functools.partial(later_kernel, tick + 1),
            (blocks, shaped(HALF, LANES, dtype=f32)),
            *shared, rows,
        )
    got = exchange(terms)
    held_rows, latest = run(
        last_sum_kernel, (piece, piece), place, got, shard, inverse, *finals
    )

    talk_rows = across_lines(held_rows, lax.axis_index("line"))
    talk_rows = exchange(replicate(talk_rows, PLACES), "place")
    payload = run(
        talk_kernel,
        shaped(2, B, block),
        place, talk_rows, latest, talk_gain, packed_own, packed_oth, embedded,
    )
    payload = jnp.broadcast_to(payload[:, None], (2, shards, B, block))
    sums = exchange(payload.reshape(2 * shards, B, block), ("core", "tp"))
    talk, leaving = run(
        finish_kernel,
        (shaped(TICKS, columns, B, dtype=f32), shaped(B, width, dtype=f32)),
        sums,
        scalars=False,
    )
    return (leaving[None], talk.transpose(0, 2, 1))


def solution(mesh):
    devices = mesh.devices
    grid = jax.sharding.Mesh(
        devices.reshape(LINES, PLACES, 2, devices.shape[1]), SECTION + ("tp",)
    )
    placed = (
        P(SECTION, None, None),
        P(SECTION, None),
        P(SECTION, None, "tp"),
        P(SECTION, "tp", None),
        P(SECTION, None, None, None, "tp"),
        P(),
        P(None, "tp"),
        P(None, "tp", SECTION),
        P(None, "tp", SECTION),
        P(),
    )
    return jax.shard_map(
        body,
        mesh=grid,
        in_specs=placed,
        out_specs=(P(SECTION, None, None), P(None, None, SECTION)),
        check_vma=False,
    )
```

```python
import functools

import jax
import jax.numpy as jnp
from jax import lax
from jax.experimental import pallas as pl
from jax.experimental.pallas import tpu as pltpu
from jax.sharding import PartitionSpec as P

D = 4096
H = 32
KVH = 8
HD = 64
NQ = 4
TICKS = 4
B = 96
CACHE = 16
HALF = B // 2
RATIO = H // KVH
EARLY = TICKS - 1
LANES = 128

epsilon = 1e-05
f32 = jnp.float32
bf16 = jnp.bfloat16
i32 = jnp.int32
CONTRACT_LAST = (((1,), (1,)), ((), ()))


def last_visible(tick, place_ref, lengths_ref):
    side, section = place_ref[0], place_ref[1]
    lens = lengths_ref[pl.ds(jnp.maximum(section - tick, 0), 1), :]
    row = lax.broadcasted_iota(i32, (HALF, B), 0)
    lane = lax.broadcasted_iota(i32, (HALF, B), 1)
    lens = jnp.where(lane == row + side * HALF, lens, 0)
    lens = jnp.sum(lens, axis=1, keepdims=True)
    ends = lens + lax.broadcasted_iota(i32, (HALF, 1), 0) * CACHE
    return jnp.concatenate([ends] * RATIO, axis=0)


def attention_terms(proj, ends, o_own, o_oth, pairs_ref, out_ref):
    shards, block = out_ref.shape[0], out_ref.shape[2] // 2
    stacked = jnp.concatenate([proj[:, r * HD : (r + 1) * HD] for r in range(RATIO)], axis=0)
    queries = (stacked.astype(bf16).astype(f32) * (HD**-0.5)).astype(bf16)
    queries = jnp.concatenate([queries, jnp.zeros_like(queries)], axis=1)
    pair_new = proj[:, RATIO * HD :].astype(bf16)
    pairs = pairs_ref[...]
    scores = lax.dot_general(queries, pairs, CONTRACT_LAST, preferred_element_type=f32)
    beside_new = jnp.concatenate([pair_new.astype(f32)] * RATIO, axis=0)
    own_scores = jnp.sum(queries.astype(f32) * beside_new, axis=-1, keepdims=True)
    rows = RATIO * HALF
    stream = lax.rem(lax.broadcasted_iota(i32, (rows, 1), 0), HALF)
    place = lax.broadcasted_iota(i32, (rows, HALF * CACHE), 1)
    visible = jnp.logical_and(place >= stream * CACHE, place < ends)
    scores = jnp.where(visible, scores, -jnp.inf)
    row_max = jnp.maximum(jnp.max(scores, axis=-1, keepdims=True), own_scores)
    weights = jnp.exp(scores - row_max)
    own_weights = jnp.exp(own_scores - row_max)
    total = jnp.sum(weights, axis=-1, keepdims=True) + own_weights
    share = 1.0 / total
    mixed = jnp.dot((weights * share).astype(bf16), pairs, preferred_element_type=f32)
    mixed = mixed + (own_weights * share).astype(bf16).astype(f32) * beside_new
    mixed = mixed[:, HD:].astype(bf16)
    heads = jnp.concatenate([mixed[r * HALF : (r + 1) * HALF] for r in range(RATIO)], axis=1)
    for j in range(shards):
        span = slice(j * block, (j + 1) * block)
        own = jnp.dot(heads, o_own[:, span], preferred_element_type=f32)
        oth = jnp.dot(heads, o_oth[:, span], preferred_element_type=f32)
        out_ref[j, :, :block] = own.astype(bf16)
        out_ref[j, :, block:] = oth.astype(bf16)


def pack_kernel(gain_ref, rows_src, adapt_src, books_src, out_ref, semaphores):
    columns, entries = adapt_src.shape[1:]
    tables = [adapt_src.at[i] for i in range(adapt_src.shape[0])]
    tables += [books_src.at[q] for q in range(NQ)]
    below = pl.ds(B, columns)
    copies = [pltpu.make_async_copy(rows_src, out_ref.at[:B], semaphores.at[0])]
    for i, source in enumerate(tables):
        target = out_ref.at[below, pl.ds(i * entries, entries)]
        copies += [pltpu.make_async_copy(source, target, semaphores.at[1 + i])]
    for copy in copies:
        copy.start()
    start = len(tables) * entries
    free = out_ref.shape[1] - start
    gain = gain_ref[...].astype(f32)
    pieces = [gain[:, j : j + free] for j in range(0, gain.shape[1], free)]
    pieces += [jnp.zeros((columns - len(pieces), free), f32)]
    out_ref[B:, start:] = jnp.concatenate(pieces, axis=0).astype(bf16)
    for copy in copies:
        copy.wait()


def unpacked_gain(packed_ref):
    width = packed_ref.shape[1]
    start = (2 + NQ) * (width // 8)
    held = packed_ref[B:, start:].astype(f32)
    count = width // (width - start)
    return jnp.concatenate([held[j : j + 1] for j in range(count)], axis=1)


def load_kernel(*refs):
    count = (len(refs) - 1) // 2
    copies = [
        pltpu.make_async_copy(refs[i], refs[count + i], refs[-1].at[i]) for i in range(count)
    ]
    for copy in copies:
        copy.start()
    for copy in copies:
        copy.wait()


def first_kernel(
    place_ref, lengths_ref, packed_own, packed_oth, w_own, w_oth, o_own, o_oth, cache_ref,
    out_ref, shard_ref, g_own_ref, g_oth_ref,
):
    side, column = place_ref[0], place_ref[2]
    block = shard_ref.shape[1] // 2
    mine = pl.ds(pl.multiple_of(side * HALF, HALF), HALF)
    own = packed_own[mine, :].astype(f32)
    oth = packed_oth[mine, :].astype(f32)
    squares = jnp.sum(own * own + oth * oth, axis=-1, keepdims=True)
    gains = [unpacked_gain(packed_own), unpacked_gain(packed_oth)]
    g_own_ref[...], g_oth_ref[...] = gains
    part = pl.ds(pl.multiple_of(column * block, block), block)
    shard_ref[:, :block] = packed_own[mine, part]
    shard_ref[:, block:] = packed_oth[mine, part]
    scaled = (own * gains[0]).astype(bf16)
    proj = jnp.dot(scaled, w_own[...], preferred_element_type=f32)
    scaled = (oth * gains[1]).astype(bf16)
    proj = proj + jnp.dot(scaled, w_oth[...], preferred_element_type=f32)
    proj = proj * lax.rsqrt(squares / D + epsilon)
    ends = last_visible(0, place_ref, lengths_ref)
    attention_terms(proj, ends, o_own, o_oth, cache_ref.at[0], out_ref)


def later_kernel(
    tick, place_ref, lengths_ref, g_own, g_oth, w_own, w_oth, o_own, o_oth, cache_ref, x_ref,
    out_ref, inverse_ref,
):
    shards, block = x_ref.shape[0], x_ref.shape[2] // 2
    squares = jnp.zeros(x_ref.shape[1:], f32)
    proj = jnp.zeros((HALF, w_own.shape[1]), f32)
    for j in range(shards):
        span = slice(j * block, (j + 1) * block)
        rows = x_ref[j].astype(f32)
        squares = squares + rows * rows
        own = (rows[:, :block] * g_own[:, span]).astype(bf16)
        oth = (rows[:, block:] * g_oth[:, span]).astype(bf16)
        proj = proj + jnp.dot(own, w_own[span, :], preferred_element_type=f32)
        proj = proj + jnp.dot(oth, w_oth[span, :], preferred_element_type=f32)
    inverse_rms = lax.rsqrt(jnp.sum(squares, axis=-1, keepdims=True) / D + epsilon)
    inverse_ref[...] = jnp.broadcast_to(inverse_rms, inverse_ref.shape)
    proj = proj * inverse_rms
    ends = last_visible(tick, place_ref, lengths_ref)
    attention_terms(proj, ends, o_own, o_oth, cache_ref.at[tick], out_ref)


def sum_kernel(tick, place_ref, got_ref, shard_ref, inverse_ref, out_ref):
    section = place_ref[1]
    shard = shard_ref[...].astype(f32)
    total = shard
    for j in range(got_ref.shape[0]):
        total = total + got_ref[j].astype(f32)
    if tick:
        passed = shard * jnp.where(section == tick - 1, inverse_ref[:, :1], 1.0)
        total = jnp.where(section >= tick, total, passed)
    out_ref[...] = total.astype(bf16)


def last_sum_kernel(
    place_ref, got_ref, shard_ref, inverse_ref, early_0, early_1, early_2, out_ref, latest_ref
):
    sum_kernel(EARLY, place_ref, got_ref, shard_ref, inverse_ref, out_ref)
    section = place_ref[1]
    latest = out_ref[...].astype(f32)
    for tick, early in ((2, early_2), (1, early_1), (0, early_0)):
        latest = jnp.where(section <= tick, early[...].astype(f32), latest)
    latest_ref[...] = latest.astype(bf16)


def pair_table(i, first, packed_own, packed_oth):
    entries = packed_own.shape[1] // 8
    span = slice(i * entries, (i + 1) * entries)
    own, oth = packed_own[B:, span].astype(f32), packed_oth[B:, span].astype(f32)
    both = [jnp.where(first, own, oth), jnp.where(first, oth, own)]
    return jnp.concatenate(both, axis=0).astype(bf16)


def embed_kernel(place_ref, packed_own, packed_oth, codes_ref, out_ref, adapt_ref):
    column, first = place_ref[2], place_ref[0] == 0
    entries = packed_own.shape[1] // 8
    embedded = jnp.zeros(out_ref.shape, f32)
    for q in range(NQ):
        ids = [codes_ref[tick, q : q + 1, :] for tick in range(TICKS)]
        ids = [jnp.where(first, row[:, :HALF], row[:, HALF:]) for row in ids]
        ids = jnp.concatenate(ids, axis=1) - column * entries
        hot = lax.broadcasted_iota(i32, (entries, TICKS * HALF), 0) == ids
        hot = jnp.where(hot, 1.0, 0.0).astype(bf16)
        table = pair_table(2 + q, first, packed_own, packed_oth)
        embedded = embedded + jnp.dot(table, hot, preferred_element_type=f32)
    out_ref[...] = embedded
    for i in range(adapt_ref.shape[0]):
        adapt_ref[i] = pair_table(i, first, packed_own, packed_oth)


def talk_kernel(
    place_ref, rows_ref, latest_ref, talk_gain, adapt_ref, embedded_ref, out_ref
):
    first = place_ref[0] == 0
    block = rows_ref.shape[2] // 2
    columns = adapt_ref.shape[1] // 2
    gains = talk_gain[...].astype(f32)

    def halves(rows):
        own, oth = rows[:, :block].astype(f32), rows[:, block:].astype(f32)
        return jnp.where(first, own, oth), jnp.where(first, oth, own)

    def beside(terms, tick):
        terms = terms[:, tick * HALF : (tick + 1) * HALF]
        return jnp.concatenate([terms[:columns], terms[columns:]], axis=1)

    embedded = embedded_ref[...]
    adapted = jnp.zeros((2 * columns, TICKS * HALF), f32)
    low, high = halves(rows_ref[...].reshape(TICKS * HALF, 2 * block))
    for i, part in enumerate((low, high)):
        scaled = (part * gains[i : i + 1]).astype(bf16)
        adapted = adapted + lax.dot_general(
            adapt_ref[i],
            scaled,
            CONTRACT_LAST,
            preferred_element_type=f32,
        )
    low, high = low[EARLY * HALF :], high[EARLY * HALF :]
    both = adapted + embedded
    pieces = [beside(both, tick) for tick in range(EARLY)]
    pieces += [beside(adapted, EARLY), beside(embedded, EARLY)]
    squares = jnp.sum(low * low + high * high, axis=1, keepdims=True)
    squares = jnp.concatenate([squares, squares], axis=0)
    upper = squares.astype(bf16).astype(f32)
    grid = jnp.concatenate(pieces, axis=0)
    grid = jnp.concatenate([grid, jnp.zeros((grid.shape[0], LANES - B), f32)], axis=1)
    grid = jnp.concatenate([grid, jnp.zeros((2 * LANES - grid.shape[0], LANES), f32)], axis=0)
    grid = grid.T[:B]
    lane = lax.broadcasted_iota(i32, grid.shape, 1)
    grid = jnp.where(lane == (TICKS + 1) * columns, upper, grid)
    grid = jnp.where(lane == (TICKS + 1) * columns + 1, squares - upper, grid)
    for c, part in enumerate(halves(latest_ref[...])):
        out_ref[c, :HALF] = grid[c * HALF : (c + 1) * HALF].astype(bf16)
        out_ref[c, HALF:] = part.astype(bf16)


def finish_kernel(got_ref, out_ref, leaving_ref):
    columns, block = out_ref.shape[1], got_ref.shape[2]
    shards = got_ref.shape[0] // 2
    tables = []
    for c in range(2):
        table = got_ref[c * shards, :HALF].astype(f32)
        for j in range(1, shards):
            table = table + got_ref[c * shards + j, :HALF].astype(f32)
        tables.append(table)
        for j in range(shards):
            rows = got_ref[c * shards + j, HALF:].astype(f32)
            leaving_ref[c * HALF : (c + 1) * HALF, j * block : (j + 1) * block] = rows
    table = jnp.concatenate(tables, axis=0)
    table = jnp.concatenate([table, jnp.zeros((LANES - B, block), f32)], axis=0).T
    for tick in range(EARLY):
        out_ref[tick] = table[tick * columns : (tick + 1) * columns, :B]
    base, at = EARLY * columns, (TICKS + 1) * columns
    squares = table[at : at + 1, :] + table[at + 1 : at + 2, :]
    rows = table[base : base + columns] * lax.rsqrt(squares / D + epsilon)
    rows = rows + table[base + columns : base + 2 * columns]
    out_ref[EARLY] = rows[:, :B]


def run(kernel, outs, *operands, scalars=True, limit=16):
    specs = [pl.BlockSpec(memory_space=pltpu.VMEM)] * len(operands)
    if scalars:
        specs[0] = pl.BlockSpec(memory_space=pltpu.SMEM)
    out_specs = jax.tree.map(lambda _: pl.BlockSpec(memory_space=pltpu.VMEM), outs)
    return pl.pallas_call(
        kernel,
        out_shape=outs,
        in_specs=specs,
        out_specs=out_specs,
        compiler_params=pltpu.CompilerParams(vmem_limit_bytes=limit * 2**20),
    )(*operands)


def shaped(*shape, dtype=bf16):
    return jax.ShapeDtypeStruct(shape, dtype)


SECTION = ("line", "place", "core")
LINES, PLACES = 8, 4
LINE = 2 * PLACES


def to_partner(value):
    return lax.ppermute(value, "core", [(0, 1), (1, 0)])


def to_next(value, tick):
    count, kept = LINES * LINE, 2 * tick
    pairs = [(i, i) for i in range(kept)] + [(i, i + 2) for i in range(kept, count - 2)]
    return lax.ppermute(value, SECTION, pairs + [(count - 2 + c, kept + c) for c in range(2)])


def exchange(blocks, axis="tp"):
    return lax.all_to_all(blocks, axis, 0, 0, tiled=True)


def replicate(block, count):
    return jnp.broadcast_to(block[None], (count,) + block.shape)


def across_lines(value, line):
    home = [LINES - 1 if place == EARLY else 0 for place in range(PLACES)]

    def sent(rows, *hops):
        at = lambda i, d: (home[i // 2] + d) % LINES * LINE + i
        pairs = [(at(i, start), at(i, end)) for start, end in hops for i in range(LINE)]
        return lax.ppermute(rows, SECTION, pairs)

    place = lax.axis_index("place")
    offset = lax.rem(line - jnp.where(place == EARLY, LINES - 1, 0) + LINES, LINES)
    some = jnp.where(offset == 0, value, jnp.zeros_like(value))
    far = sent(value, (0, 4))
    some = some + sent(value, (0, 7)) + sent(value, (0, 1))
    return some + sent(some, (1, 2), (7, 6)) + sent(some, (1, 3), (7, 5)) + far


def body(arriving, norm_gain, w_qkv, w_out, cache, lengths, talk_gain, w_adapt, codebooks, codes):
    position = lax.axis_index(SECTION)
    column = lax.axis_index("tp")
    shards = lax.axis_size("tp")
    section = position // 2
    width = arriving.shape[2]
    block = width // shards
    columns = w_adapt.shape[2]
    place = jnp.stack([lax.rem(position, 2), section, column]).astype(i32)

    w_own, o_own = w_qkv[0], w_out[0]
    w_oth = to_partner(w_own)
    o_oth = to_partner(o_own)
    there = pl.BlockSpec(memory_space=pltpu.HBM)
    here = pl.BlockSpec(memory_space=pltpu.VMEM)
    sources = [arriving[0], w_adapt.transpose(0, 2, 1), codebooks.transpose(0, 2, 1)]
    packed_own = pl.pallas_call(
        pack_kernel,
        out_shape=shaped(B + columns, width),
        in_specs=[here] + [there] * len(sources),
        out_specs=here,
        scratch_shapes=[pltpu.SemaphoreType.DMA((3 + NQ,))],
        compiler_params=pltpu.CompilerParams(vmem_limit_bytes=8 * 2**20),
    )(norm_gain, *(pltpu.with_memory_space_constraint(v, pltpu.HBM) for v in sources))
    packed_oth = to_partner(packed_own)
    cache_rows = cache[0].reshape(TICKS, HALF * CACHE, -1)
    blocks = shaped(shards, HALF, 2 * block)
    piece = shaped(HALF, 2 * block)

    sources, _ = lax.optimization_barrier(([lengths, w_own, o_own, cache_rows], packed_own))
    lengths, w_own, o_own, cache_rows = pl.pallas_call(
        load_kernel,
        out_shape=tuple(shaped(*v.shape, dtype=v.dtype) for v in sources),
        in_specs=[there] * len(sources),
        out_specs=(here,) * len(sources),
        scratch_shapes=[pltpu.SemaphoreType.DMA((len(sources),))],
        compiler_params=pltpu.CompilerParams(vmem_limit_bytes=8 * 2**20),
        cost_estimate=pl.CostEstimate(flops=0, bytes_accessed=7 * 2**20, transcendentals=0),
    )(*(pltpu.with_memory_space_constraint(v, pltpu.HBM) for v in sources))
    weights = (w_own, w_oth, o_own, o_oth, cache_rows)
    gain = shaped(1, width, dtype=f32)
    terms, shard, g_own, g_oth = run(
        first_kernel, (blocks, piece, gain, gain), place, lengths, packed_own, packed_oth, *weights
    )
    shared = (place, lengths, g_own, g_oth, *weights)
    finals = []
    inverse = jnp.zeros((HALF, LANES), f32)
    for tick in range(EARLY):
        got = exchange(terms)
        finals.append(run(functools.partial(sum_kernel, tick), piece, place, got, shard, inverse))
        shard = to_next(finals[-1], tick)
        if tick == 0:
            tokens, _ = lax.optimization_barrier((codes.transpose(0, 2, 1), finals[0]))
            embedded, adapt = run(
                embed_kernel,
                (shaped(2 * columns, TICKS * HALF, dtype=f32), shaped(2, 2 * columns, block)),
                place, packed_own, packed_oth, tokens,
            )
            shard, embedded, adapt = lax.optimization_barrier((shard, embedded, adapt))
        rows = exchange(replicate(shard, shards))
        terms, inverse = run(
            functools.partial(later_kernel, tick + 1),
            (blocks, shaped(HALF, LANES, dtype=f32)),
            *shared, rows,
        )
    got = exchange(terms)
    held_rows, latest = run(
        last_sum_kernel, (piece, piece), place, got, shard, inverse, *finals
    )

    talk_rows = across_lines(held_rows, lax.axis_index("line"))
    talk_rows = exchange(replicate(talk_rows, PLACES), "place")
    payload = run(
        talk_kernel,
        shaped(2, B, block),
        place, talk_rows, latest, talk_gain, adapt, embedded,
    )
    payload = jnp.broadcast_to(payload[:, None], (2, shards, B, block))
    sums = exchange(payload.reshape(2 * shards, B, block), ("core", "tp"))
    talk, leaving = run(
        finish_kernel,
        (shaped(TICKS, columns, B, dtype=f32), shaped(B, width, dtype=f32)),
        sums,
        scalars=False,
    )
    return (leaving[None], talk.transpose(0, 2, 1))


def solution(mesh):
    devices = mesh.devices
    grid = jax.sharding.Mesh(
        devices.reshape(LINES, PLACES, 2, devices.shape[1]), SECTION + ("tp",)
    )
    placed = (
        P(SECTION, None, None),
        P(SECTION, None),
        P(SECTION, None, "tp"),
        P(SECTION, "tp", None),
        P(SECTION, None, None, None, "tp"),
        P(),
        P(None, "tp"),
        P(None, "tp", SECTION),
        P(None, "tp", SECTION),
        P(),
    )
    return jax.shard_map(
        body,
        mesh=grid,
        in_specs=placed,
        out_specs=(P(SECTION, None, None), P(None, None, SECTION)),
        check_vma=False,
    )
```
